256 devices in a mesh: head: 8 (over y, core), inner: 2 (over z_hi), outer: 16 (over z_lo, x).
Axes of the slice: x: 4, y: 4, z: 8 (z_hi: 2, z_lo: 4; z = z_hi * 4 + z_lo), core: 2. Of those that a mesh axis runs over, the one named last changes fastest.
Arguments:
- query: bfloat16 [16384, 48, 128], P(('head', 'inner', 'outer')), may hold values from -6 to 6
- keys: bfloat16 [16384, 8, 128], P(('head', 'inner', 'outer')), may hold values from -6 to 6
- values: bfloat16 [16384, 8, 128], P(('head', 'inner', 'outer')), may hold values from -6 to 6
- attn_out: bfloat16 [16384, 48, 128], P(('head', 'inner', 'outer')), may hold values from -1.5 to 1.5
- grad_out: bfloat16 [16384, 48, 128], P(('head', 'inner', 'outer')), may hold values from -6 to 6
- log_norm: float32 [16384, 48], P(('head', 'inner', 'outer'))
- block_order: int32 [256], replicated, may hold values from 0 to 255, as said below
Outputs:
- grad_query: bfloat16 [16384, 48, 128], P(('head', 'inner', 'outer'))
- grad_keys: bfloat16 [16384, 8, 128], P(('head', 'inner', 'outer'))
- grad_values: bfloat16 [16384, 8, 128], P(('head', 'inner', 'outer'))
The draws below stay inside these ranges and needn't reach their ends.
Inputs may be any that keep to these rules, and one draw needn't show every extreme that they name: `block_order`: each place of the sequence's 256 blocks appears once.
All inputs are finite; a program needn't handle non-finite values.
Results may differ from the reference program's by a relative error of at most 0.0056.
Values may be sent and summed in bfloat16 or wider, within the bound.
No kernel may reach another device: no remote copies, remote signals or barrier semaphores. Data moves between devices by JAX's collectives and lax.ppermute only.
A program may use at most 128 MiB of HBM per device.

```python
import jax
import jax.numpy as jnp
from jax import lax

QUERY_HEADS = 48
KEY_VALUE_HEADS = 8
HEAD_SIZE = 128
TOK_DEV = 64
SEQUENCE_TOKENS = 16384
NBLK = 256
WINDOW = 2048
N_HEAD = 8
N_INNER = 2
N_OUTER = 16


def shared_order(key):
    return jax.random.permutation(key, NBLK).astype(jnp.int32)


def draw_block_order(key, part):
    order = shared_order(key)
    return order


def draw_log_norm(key, part):
    order = shared_order(key)
    key = jax.random.fold_in(key, 7)
    rows = jnp.arange(SEQUENCE_TOKENS, dtype=jnp.int32)
    position = order[rows // TOK_DEV] * TOK_DEV + rows % TOK_DEV
    base = 0.5 * jnp.log(WINDOW * (position.astype(jnp.float32) + 1.0) / SEQUENCE_TOKENS + 1.0) + 1.5
    noise = jax.random.uniform(key, (SEQUENCE_TOKENS, QUERY_HEADS), jnp.float32, -0.3, 0.3)
    return (base[:, None] + noise).astype(jnp.float32)


def levels(key, dims, shards, low, high):
    def one(axis_at, parts):
        steps = jax.random.uniform(jax.random.fold_in(jax.random.fold_in(key, 6), axis_at), (parts,), jnp.float32, low / len(shards), high / len(shards))
        return jnp.repeat(jnp.exp(steps), dims[axis_at] // parts).reshape((-1,) + (1,) * (len(dims) - axis_at - 1))

    factor_of = one(*shards[0])
    for cut in shards[1:]:
        factor_of = factor_of * one(*cut)
    return factor_of


def scatter_about(own_key, dims, scale, most, cuts=(), held_as=jnp.bfloat16):
    level = levels(own_key, dims, cuts, -0.22, 0.18) if cuts else 1.0
    values = jax.random.normal(own_key, dims, jnp.float32) * scale * level
    return jnp.minimum(jnp.maximum(values, -most), most).astype(held_as)


def setup_inputs(seed: int = 0) -> dict:
    streams_of = jax.random.split(jax.random.key(seed), 8)
    query = scatter_about(streams_of[0], (SEQUENCE_TOKENS, QUERY_HEADS, HEAD_SIZE), 1.0, 6.0, ((0, 256),))
    keys = scatter_about(streams_of[1], (SEQUENCE_TOKENS, KEY_VALUE_HEADS, HEAD_SIZE), 1.0, 6.0, ((0, 256),))
    values = scatter_about(streams_of[2], (SEQUENCE_TOKENS, KEY_VALUE_HEADS, HEAD_SIZE), 1.0, 6.0, ((0, 256),))
    attn_out = scatter_about(streams_of[3], (SEQUENCE_TOKENS, QUERY_HEADS, HEAD_SIZE), 0.25, 1.5, ((0, 256),))
    grad_out = scatter_about(streams_of[4], (SEQUENCE_TOKENS, QUERY_HEADS, HEAD_SIZE), 1.0, 6.0, ((0, 256),))
    log_norm = draw_log_norm(jax.random.fold_in(streams_of[7], 71), 0)
    block_order = draw_block_order(jax.random.fold_in(streams_of[7], 71), 0)
    return {"query": query, "keys": keys, "values": values, "attn_out": attn_out, "grad_out": grad_out, "log_norm": log_norm, "block_order": block_order}


def arrange(array):
    rest = array.shape[1:]
    shaped = array.reshape((N_HEAD, N_INNER, N_OUTER, TOK_DEV) + rest)
    shaped = jnp.moveaxis(shaped, 0, 2)
    return shaped.reshape((N_INNER, N_OUTER, N_HEAD * TOK_DEV) + rest)


def restore(array):
    rest = array.shape[3:]
    shaped = array.reshape((N_INNER, N_OUTER, N_HEAD, TOK_DEV) + rest)
    shaped = jnp.moveaxis(shaped, 2, 0)
    return shaped.reshape((N_HEAD * N_INNER * N_OUTER * TOK_DEV,) + rest)


def reference(query, keys, values, attn_out, grad_out, log_norm, block_order):
    seq = query.shape[0]
    scale = HEAD_SIZE ** -0.5
    query_group_size = QUERY_HEADS // KEY_VALUE_HEADS
    context_rows = N_HEAD * TOK_DEV
    cycle_len = N_INNER * N_OUTER
    rows = jnp.arange(seq, dtype=jnp.int32)
    position = (block_order[rows // TOK_DEV] * TOK_DEV + rows % TOK_DEV).astype(jnp.int32)
    delta = jnp.sum(grad_out.astype(jnp.float32) * attn_out.astype(jnp.float32), axis=-1)
    query_full = arrange(query)
    output_gradient_full = arrange(grad_out)
    k_all = arrange(keys)
    v_all = arrange(values)
    logsumexp_full = arrange(log_norm)
    delta_everywhere = arrange(delta)
    pos_all = arrange(position)

    def band(array, outer_at):
        near = lax.dynamic_index_in_dim(array, outer_at, 1, keepdims=False)
        far = lax.dynamic_index_in_dim(array, (outer_at - 1) % N_OUTER, 1, keepdims=False)
        both = jnp.stack([near, far], axis=0)
        return both.reshape((2 * N_INNER * context_rows,) + array.shape[3:])

    def step(carry, context):
        dk_total, dv_total = carry
        inner_at = (context // N_OUTER).astype(jnp.int32)
        outer_at = (context % N_OUTER).astype(jnp.int32)
        far_at = ((outer_at - 1) % N_OUTER).astype(jnp.int32)

        def select_rows(array):
            row = lax.dynamic_index_in_dim(array, inner_at, 0, keepdims=False)
            return lax.dynamic_index_in_dim(row, outer_at, 0, keepdims=False)

        query_row_slice = select_rows(query_full).astype(jnp.float32).reshape(context_rows, KEY_VALUE_HEADS, query_group_size, HEAD_SIZE)
        output_gradient_rows = select_rows(output_gradient_full).astype(jnp.float32).reshape(context_rows, KEY_VALUE_HEADS, query_group_size, HEAD_SIZE)
        logsumexp_rows = select_rows(logsumexp_full).reshape(context_rows, KEY_VALUE_HEADS, query_group_size).transpose(1, 2, 0)[..., None]
        delta_row_slice = select_rows(delta_everywhere).reshape(context_rows, KEY_VALUE_HEADS, query_group_size).transpose(1, 2, 0)[..., None]
        pos_rows = select_rows(pos_all)
        k_band = band(k_all, outer_at).astype(jnp.float32)
        v_band = band(v_all, outer_at).astype(jnp.float32)
        pos_band = band(pos_all, outer_at)
        score = jnp.einsum("tkgd,ukd->kgtu", query_row_slice, k_band) * scale
        allowed = pos_band[None, :] <= pos_rows[:, None]
        prob = jnp.exp(jnp.where(allowed, score - logsumexp_rows, -1e30))
        weight = prob.astype(jnp.bfloat16).astype(jnp.float32)
        value_gradient_part = jnp.einsum("kgtu,tkgd->ukd", weight, output_gradient_rows)
        dprob = jnp.einsum("tkgd,ukd->kgtu", output_gradient_rows, v_band)
        dscore = (prob * (dprob - delta_row_slice)).astype(jnp.bfloat16).astype(jnp.float32)
        dq_rows = (scale * jnp.einsum("kgtu,ukd->tkgd", dscore, k_band)).astype(jnp.bfloat16)
        key_gradient_part = jnp.einsum("kgtu,tkgd->ukd", dscore, query_row_slice)
        key_gradient_part = key_gradient_part.reshape(2, N_INNER, context_rows, KEY_VALUE_HEADS, HEAD_SIZE)
        value_gradient_part = value_gradient_part.reshape(2, N_INNER, context_rows, KEY_VALUE_HEADS, HEAD_SIZE)
        dk_total = dk_total.at[:, outer_at].add(key_gradient_part[0]).at[:, far_at].add(key_gradient_part[1])
        dv_total = dv_total.at[:, outer_at].add(value_gradient_part[0]).at[:, far_at].add(value_gradient_part[1])
        return (dk_total, dv_total), dq_rows.reshape(context_rows, QUERY_HEADS, HEAD_SIZE)

    zero_filled = jnp.zeros((N_INNER, N_OUTER, context_rows, KEY_VALUE_HEADS, HEAD_SIZE), jnp.float32)
    (dk_total, dv_total), dq_blocks = lax.scan(step, (zero_filled, zero_filled), jnp.arange(cycle_len, dtype=jnp.int32))
    grad_query = restore(dq_blocks.reshape(N_INNER, N_OUTER, context_rows, QUERY_HEADS, HEAD_SIZE))
    grad_keys = restore((scale * dk_total).astype(jnp.bfloat16))
    grad_values = restore(dv_total.astype(jnp.bfloat16))
    return (grad_query, grad_keys, grad_values)
```

```python
import math

import jax
import jax.numpy as jnp
from jax import lax
from jax.experimental import pallas as pl
from jax.experimental.pallas import tpu as pltpu
from jax.sharding import PartitionSpec as P

LOG2E = math.log2(math.e)
NT = (((1,), (1,)), ((), ()))
NN = (((1,), (0,)), ((), ()))
TN = (((0,), (0,)), ((), ()))
f32 = jnp.float32
bf16 = jnp.bfloat16


def attention_part(tables, packed, kv_own, kv_partner, dq_start, keys_step, rows_step, name):
    src, parts, T, D = packed.shape
    heads = (parts - 1) // 2
    R = heads * T
    n = 2 * src
    U, W = keys_step * T, rows_step * R
    groups = n // keys_step
    scale = D ** (-0.5)
    lanes = R // D
    last = dq_start is not None

    def body(qid, qord, kid, kord, cnt, packed_ref, own_ref, partner_ref, *rest):
        if last:
            start_ref, dq_ref, gown_ref, gpartner_ref, *scratch = rest
            q_s, do_s, st_s, kv_s, g_s, k_s, v_s, dk_s, dv_s, dq_s = scratch
            dq_s[...] = start_ref[...]
        else:
            dq_s, gown_ref, gpartner_ref, *scratch = rest
            q_s, do_s, st_s, kv_s, g_s, k_s, v_s, dk_s, dv_s = scratch
            dq_s[...] = jnp.zeros_like(dq_s)
        kv_s[0:src] = own_ref[...]
        kv_s[src:n] = partner_ref[...]

        def prepare(i, carry):
            b = qid[i]
            at = pl.ds(pl.multiple_of(i * R, R), R)
            q_s[at] = packed_ref[b, 0:heads].reshape(R, D)
            do_s[at] = packed_ref[b, heads : 2 * heads].reshape(R, D)
            st = packed_ref[b, 2 * heads].astype(f32)
            st = st[0:8] + st[8:16] + st[16:24]
            st_s[i, 0:1] = jnp.concatenate([st[j : j + 1] for j in range(lanes)], axis=1)
            st_s[i, 1:2] = jnp.concatenate([st[j : j + 1] for j in range(lanes, 2 * lanes)], axis=1)
            return carry

        lax.fori_loop(0, src, prepare, 0)
        lead = lax.broadcasted_iota(jnp.int32, (T, R), 1) % T - lax.broadcasted_iota(
            jnp.int32, (T, R), 0
        )

        def group(g, carry):
            for j in range(keys_step):
                b = kid[g * keys_step + j]
                k_s[pl.ds(j * T, T)] = kv_s[b, 0]
                v_s[pl.ds(j * T, T)] = kv_s[b, 1]
            dk_s[...] = jnp.zeros_like(dk_s)
            dv_s[...] = jnp.zeros_like(dv_s)

            def step(i, inner):
                at = pl.ds(pl.multiple_of(i * W, W), W)
                q, do, k, v = q_s[at], do_s[at], k_s[...], v_s[...]
                s = lax.dot_general(k, q, NT, preferred_element_type=f32)
                dp = lax.dot_general(v, do, NT, preferred_element_type=f32)
                p_cols, ds_cols = [], []
                for h in range(rows_step):
                    row = i * rows_step + h
                    lse, delta, place = st_s[row, 0:1], st_s[row, 1:2], qord[row]
                    p_rows, ds_rows = [], []
                    for j in range(keys_step):
                        behind = (kord[g * keys_step + j] - place) * T
                        cut = (slice(j * T, (j + 1) * T), slice(h * R, (h + 1) * R))
                        p = jnp.where(
                            lead >= behind, jnp.exp2(s[cut] * (scale * LOG2E) - lse), 0.0
                        )
                        ds_rows.append((p * (dp[cut] - delta)).astype(bf16))
                        p_rows.append(p.astype(bf16))
                    p_cols.append(jnp.concatenate(p_rows, axis=0))
                    ds_cols.append(jnp.concatenate(ds_rows, axis=0))
                p, ds = jnp.concatenate(p_cols, axis=1), jnp.concatenate(ds_cols, axis=1)
                dv_s[...] += lax.dot_general(p, do, NN, preferred_element_type=f32)
                dk_s[...] += lax.dot_general(ds, q, NN, preferred_element_type=f32)
                dq_s[at] += lax.dot_general(ds, k, TN, preferred_element_type=f32)
                return inner

            lax.fori_loop(0, cnt[g], step, 0)
            for j in range(keys_step):
                b = kid[g * keys_step + j]
                g_s[b, 0] = (dk_s[pl.ds(j * T, T)] * scale).astype(g_s.dtype)
                g_s[b, 1] = dv_s[pl.ds(j * T, T)].astype(g_s.dtype)
            return carry

        lax.fori_loop(0, groups, group, 0)
        gown_ref[...] = g_s[0:src]
        gpartner_ref[...] = g_s[src:n]
        if last:

            def finish(i, carry):
                at = pl.ds(pl.multiple_of(i * R, R), R)
                dq_ref[qid[i]] = (dq_s[at] * scale).astype(bf16).reshape(heads, T, D)
                return carry

            lax.fori_loop(0, src, finish, 0)

    smem = pl.BlockSpec(memory_space=pltpu.SMEM)
    vmem = pl.BlockSpec(memory_space=pltpu.VMEM)
    dq_f32 = jax.ShapeDtypeStruct((src * R, D), f32)
    dq_out = jax.ShapeDtypeStruct((src, heads, T, D), bf16) if last else dq_f32
    g_type = f32 if last else bf16
    g_out = jax.ShapeDtypeStruct((src, 2, T, D), g_type)
    scratch = [
        pltpu.VMEM((src * R, D), bf16),
        pltpu.VMEM((src * R, D), bf16),
        pltpu.VMEM((src, 8, R), f32),
        pltpu.VMEM((n, 2, T, D), bf16),
        pltpu.VMEM((n, 2, T, D), g_type),
        pltpu.VMEM((U, D), bf16),
        pltpu.VMEM((U, D), bf16),
        pltpu.VMEM((U, D), f32),
        pltpu.VMEM((U, D), f32),
    ]
    arrays = [packed, kv_own, kv_partner]
    if last:
        scratch.append(pltpu.VMEM((src * R, D), f32))
        arrays.append(dq_start)
    return pl.pallas_call(
        body,
        out_shape=(dq_out, g_out, g_out),
        in_specs=[smem] * 5 + [vmem] * len(arrays),
        out_specs=(vmem,) * 3,
        scratch_shapes=scratch,
        compiler_params=pltpu.CompilerParams(vmem_limit_bytes=48 * 2**20),
        cost_estimate=pl.CostEstimate(
            flops=10 * src * R * n * T * D, bytes_accessed=6 * 2**20, transcendentals=src * R * n * T
        ),
        name=name,
    )(*tables, *arrays)


def sort_down(order):
    ids = jnp.arange(order.shape[0], dtype=jnp.int32)
    rank = jnp.sum((order[None, :] > order[:, None]).astype(jnp.int32), axis=1)
    hit = rank[None, :] == ids[:, None]
    return (
        jnp.sum(jnp.where(hit, ids[None, :], 0), axis=1),
        jnp.sum(jnp.where(hit, order[None, :], 0), axis=1),
    )


def pieces(x):
    high = lax.reduce_precision(x, 8, 7)
    rest = x - high
    middle = lax.reduce_precision(rest, 8, 7)
    return [v.astype(bf16) for v in (high, middle, rest - middle)]


def shards(query, keys, values, attn_out, grad_out, log_norm, block_order):
    heads = lax.axis_size("head")
    inners = lax.axis_size("inner")
    outers = lax.axis_size("outer")
    T, q_heads, D = query.shape
    group = q_heads // keys.shape[1]
    i, o = lax.axis_index("inner"), lax.axis_index("outer")

    ring = ("inner", "outer")
    place = lambda a, b: a * outers + b
    swap = [(place(1 - a, b), place(a, b)) for a in range(inners) for b in range(outers)]
    ahead = [
        (place(a, b), place(a, b + 1) if b + 1 < outers else place(1 - a, 0))
        for a in range(inners)
        for b in range(outers)
    ]
    back = [(b, a) for a, b in ahead]

    def exchange(x):
        return lax.all_to_all(x, "head", split_axis=0, concat_axis=0, tiled=True)

    def by_head(x):
        return x.reshape(T, heads, -1, D).transpose(1, 2, 0, 3)

    kv = exchange(jnp.concatenate([by_head(keys), by_head(values)], axis=1))
    kv_partner = lax.ppermute(kv, ring, swap)
    kv_far = lax.ppermute(kv, ring, ahead)
    kv_far_partner = lax.ppermute(kv_partner, ring, ahead)

    delta = jnp.sum(grad_out.astype(f32) * attn_out.astype(f32), axis=-1)
    stats = jnp.stack([log_norm * LOG2E, delta])
    lanes = group * T // D
    stats = stats.reshape(2, T, heads, group).transpose(2, 0, 3, 1).reshape(heads, 2 * lanes, D)
    stats = jnp.pad(stats, ((0, 0), (0, 8 - 2 * lanes), (0, 0)))
    stats = jnp.concatenate(pieces(stats), axis=1)
    stats = jnp.pad(stats, ((0, 0), (0, T - 24), (0, 0)))
    packed = exchange(
        jnp.concatenate([by_head(query), by_head(grad_out), stats[:, None]], axis=1)
    )

    table = block_order.reshape(heads, inners, outers)

    def places(a, b):
        return lax.dynamic_slice(table, (0, a, b), (heads, 1, 1)).reshape(heads)

    keys_step, rows_step = 8, 2
    q_id, q_order = sort_down(places(i, o))
    before = (o - 1) % outers
    turn = jnp.where(o == 0, 1 - i, i)

    def tables(a, b):
        k_id, k_order = sort_down(jnp.concatenate([places(a, b), places(1 - a, b)]))
        least = k_order.reshape(-1, keys_step)[:, -1]
        seen = jnp.sum((q_order[None, :] >= least[:, None]).astype(jnp.int32), axis=1)
        return q_id, q_order, k_id, k_order, (seen + rows_step - 1) // rows_step

    dq, far, far_partner = attention_part(
        tables(turn, before), packed, kv_far, kv_far_partner, None, keys_step, rows_step, "far_keys"
    )
    far_partner = lax.ppermute(far_partner, ring, back)
    far = lax.ppermute(far, ring, back)
    dq, near, near_partner = attention_part(
        tables(i, o), packed, kv, kv_partner, dq, keys_step, rows_step, "near_keys"
    )
    dq = exchange(dq)
    partner = lax.ppermute((near_partner + far_partner.astype(f32)).astype(bf16), ring, swap)
    grad = exchange((near + far.astype(f32) + partner.astype(f32)).astype(bf16))
    grad = grad.transpose(1, 2, 0, 3)
    return dq.reshape(q_heads, T, D).transpose(1, 0, 2), grad[0], grad[1]


def solution(mesh):
    rows = P(("head", "inner", "outer"))
    return jax.shard_map(
        shards,
        mesh=mesh,
        in_specs=(rows,) * 6 + (P(),),
        out_specs=(rows,) * 3,
        check_vma=False,
    )
```

```python
import math

import jax
import jax.numpy as jnp
from jax import lax
from jax.experimental import pallas as pl
from jax.experimental.pallas import tpu as pltpu
from jax.sharding import PartitionSpec as P

LOG2E = math.log2(math.e)
NT = (((1,), (1,)), ((), ()))
NN = (((1,), (0,)), ((), ()))
f32 = jnp.float32
bf16 = jnp.bfloat16


def attention_part(tables, packed, contexts, dq_start, last, keys_step, rows_step, g_types, name):
    src, parts, T, D = packed.shape
    heads = (parts - 1) // 2
    R = heads * T
    many = len(contexts)
    n = many * src
    U, W = keys_step * T, rows_step * R
    groups = n // keys_step
    scale = D ** (-0.5)
    lanes = R // D
    first = dq_start is None

    def body(qid, qord, kid, kord, cnt, packed_ref, *rest):
        kv_refs, rest = rest[:many], rest[many:]
        if not first:
            start_ref, *rest = rest
        out_ref, *rest = rest
        g_refs, rest = rest[:many], rest[many:]
        if many > 1:
            kv_s, g_s, *rest = rest
            for c in range(many):
                kv_s[c * src : (c + 1) * src] = kv_refs[c][...]
        else:
            kv_s, g_s = kv_refs[0], g_refs[0]
        st_s, k_s, v_s, kt_s, dk_s, dv_s, *rest = rest
        dq_s = rest[0] if last else out_ref
        dq_s[...] = jnp.zeros_like(dq_s) if first else start_ref[...]

        def prepare(i, carry):
            st = packed_ref[qid[i], 2 * heads].astype(f32)
            st = st[0:8] + st[8:16] + st[16:24]
            st_s[i, 0:1] = jnp.concatenate([st[j : j + 1] for j in range(lanes)], axis=1)
            st_s[i, 1:2] = jnp.concatenate([st[j : j + 1] for j in range(lanes, 2 * lanes)], axis=1)
            return carry

        lax.fori_loop(0, src, prepare, 0)
        lead = lax.broadcasted_iota(jnp.int32, (T, R), 1) % T - lax.broadcasted_iota(
            jnp.int32, (T, R), 0
        )

        def group(g, carry):
            for j in range(keys_step):
                b = kid[g * keys_step + j]
                k_s[pl.ds(j * T, T)] = kv_s[b, 0]
                v_s[pl.ds(j * T, T)] = kv_s[b, 1]
            kt_s[...] = k_s[...].T
            dk_s[...] = jnp.zeros_like(dk_s)
            dv_s[...] = jnp.zeros_like(dv_s)

            def step(i, inner):
                at = pl.ds(pl.multiple_of(i * W, W), W)
                ids = [qid[i * rows_step + h] for h in range(rows_step)]
                q = jnp.concatenate([packed_ref[b, 0:heads].reshape(R, D) for b in ids], axis=0)
                do = jnp.concatenate(
                    [packed_ref[b, heads : 2 * heads].reshape(R, D) for b in ids], axis=0
                )
                k, v = k_s[...], v_s[...]
                s = lax.dot_general(k, q, NT, preferred_element_type=f32)
                dp = lax.dot_general(v, do, NT, preferred_element_type=f32)
                p_cols, ds_cols = [], []
                for h in range(rows_step):
                    row = i * rows_step + h
                    lse, delta, place = st_s[row, 0:1], st_s[row, 1:2], qord[row]
                    p_rows, ds_rows = [], []
                    for j in range(keys_step):
                        behind = (kord[g * keys_step + j] - place) * T
                        cut = (slice(j * T, (j + 1) * T), slice(h * R, (h + 1) * R))
                        p = jnp.where(
                            lead >= behind, jnp.exp2(s[cut] * (scale * LOG2E) - lse), 0.0
                        )
                        ds_rows.append((p * (dp[cut] - delta)).astype(bf16))
                        p_rows.append(p.astype(bf16))
                    p_cols.append(jnp.concatenate(p_rows, axis=0))
                    ds_cols.append(jnp.concatenate(ds_rows, axis=0))
                p, ds = jnp.concatenate(p_cols, axis=1), jnp.concatenate(ds_cols, axis=1)
                dv_s[...] += lax.dot_general(p, do, NN, preferred_element_type=f32)
                dk_s[...] += lax.dot_general(ds, q, NN, preferred_element_type=f32)
                dq_s[:, at] += lax.dot_general(kt_s[...], ds, NN, preferred_element_type=f32)
                return inner

            lax.fori_loop(0, cnt[g], step, 0)
            for j in range(keys_step):
                b = kid[g * keys_step + j]
                g_s[b, 0] = (dk_s[pl.ds(j * T, T)] * scale).astype(g_s.dtype)
                g_s[b, 1] = dv_s[pl.ds(j * T, T)].astype(g_s.dtype)
            return carry

        lax.fori_loop(0, groups, group, 0)
        if many > 1:
            for c in range(many):
                g_refs[c][...] = g_s[c * src : (c + 1) * src].astype(g_refs[c].dtype)
        if last:
            for j in range(src):
                at = pl.ds(j * R, R)
                out_ref[qid[j]] = (dq_s[:, at].T * scale).astype(bf16).reshape(heads, T, D)

    smem = pl.BlockSpec(memory_space=pltpu.SMEM)
    vmem = pl.BlockSpec(memory_space=pltpu.VMEM)
    if last:
        dq_out = jax.ShapeDtypeStruct((src, heads, T, D), bf16)
    else:
        dq_out = jax.ShapeDtypeStruct((D, src * R), f32)
    g_outs = [jax.ShapeDtypeStruct((src, 2, T, D), t) for t in g_types]
    scratch = []
    if many > 1:
        scratch = [pltpu.VMEM((n, 2, T, D), bf16), pltpu.VMEM((n, 2, T, D), f32)]
    scratch += [
        pltpu.VMEM((src, 8, R), f32),
        pltpu.VMEM((U, D), bf16),
        pltpu.VMEM((U, D), bf16),
        pltpu.VMEM((D, U), bf16),
        pltpu.VMEM((U, D), f32),
        pltpu.VMEM((U, D), f32),
    ]
    if last:
        scratch.append(pltpu.VMEM((D, src * R), f32))
    arrays = [packed, *contexts] + ([] if first else [dq_start])
    return pl.pallas_call(
        body,
        out_shape=(dq_out, *g_outs),
        in_specs=[smem] * 5 + [vmem] * len(arrays),
        out_specs=(vmem,) * (1 + many),
        scratch_shapes=scratch,
        compiler_params=pltpu.CompilerParams(vmem_limit_bytes=32 * 2**20),
        cost_estimate=pl.CostEstimate(flops=1, bytes_accessed=1, transcendentals=0),
        name=name,
    )(*tables, *arrays)


def add_by_peer(me, *arrays):
    src, *rest = arrays[0].shape

    def body(me_ref, *refs):
        ins, outs = refs[: len(arrays)], refs[len(arrays) :]
        for j in range(src):
            at = me_ref[0] ^ j
            outs[j][...] = sum(r[at].astype(f32) for r in ins).astype(bf16)

    smem = pl.BlockSpec(memory_space=pltpu.SMEM)
    vmem = pl.BlockSpec(memory_space=pltpu.VMEM)
    return pl.pallas_call(
        body,
        out_shape=[jax.ShapeDtypeStruct(rest, bf16)] * src,
        in_specs=[smem] + [vmem] * len(arrays),
        out_specs=[vmem] * src,
        cost_estimate=pl.CostEstimate(flops=10**10, bytes_accessed=1, transcendentals=0),
        name="add_by_peer",
    )(me.reshape(1), *arrays)


def gather_grads(me, pieces):
    src = len(pieces)
    _, T, D = pieces[0].shape

    def body(me_ref, *refs):
        ins, outs, held, wide = refs[:src], refs[src : src + 2], refs[-2], refs[-1]
        for j in range(src):
            held[me_ref[0] ^ j] = ins[j][...]
        for c in range(2):
            for g in range(src):
                wide[:, g, :] = held[g, c].astype(f32)
            outs[c][...] = wide[...].astype(bf16)

    smem = pl.BlockSpec(memory_space=pltpu.SMEM)
    vmem = pl.BlockSpec(memory_space=pltpu.VMEM)
    return pl.pallas_call(
        body,
        out_shape=[jax.ShapeDtypeStruct((T, src, D), bf16)] * 2,
        in_specs=[smem] + [vmem] * src,
        out_specs=[vmem] * 2,
        scratch_shapes=[pltpu.VMEM((src, 2, T, D), bf16), pltpu.VMEM((T, src, D), f32)],
        name="gather_grads",
    )(me.reshape(1), *pieces)


def sort_down(order):
    ids = jnp.arange(order.shape[0], dtype=jnp.int32)
    rank = jnp.sum((order[None, :] > order[:, None]).astype(jnp.int32), axis=1)
    hit = rank[None, :] == ids[:, None]
    return (
        jnp.sum(jnp.where(hit, ids[None, :], 0), axis=1),
        jnp.sum(jnp.where(hit, order[None, :], 0), axis=1),
    )


def pieces(x):
    high = lax.reduce_precision(x, 8, 7)
    rest = x - high
    middle = lax.reduce_precision(rest, 8, 7)
    return [v.astype(bf16) for v in (high, middle, rest - middle)]


def shards(query, keys, values, attn_out, grad_out, log_norm, block_order):
    heads = lax.axis_size("head")
    inners = lax.axis_size("inner")
    outers = lax.axis_size("outer")
    T, q_heads, D = query.shape
    group = q_heads // keys.shape[1]
    i, o = lax.axis_index("inner"), lax.axis_index("outer")

    ring = ("inner", "outer")
    place = lambda a, b: a * outers + b
    swap = [(place(1 - a, b), place(a, b)) for a in range(inners) for b in range(outers)]
    ahead = [
        (place(a, b), place(a, b + 1) if b + 1 < outers else place(1 - a, 0))
        for a in range(inners)
        for b in range(outers)
    ]
    back = [(b, a) for a, b in ahead]

    def exchange(x):
        return lax.all_to_all(x, "head", split_axis=0, concat_axis=0, tiled=True)

    def by_head(x):
        return x.reshape(T, heads, -1, D).transpose(1, 2, 0, 3)

    kv = exchange(jnp.concatenate([by_head(keys), by_head(values)], axis=1))
    kv_partner = lax.ppermute(kv, ring, swap)
    kv_far = lax.ppermute(kv, ring, ahead)
    kv_far_partner = lax.ppermute(kv_partner, ring, ahead)

    delta = jnp.sum(grad_out.astype(f32) * attn_out.astype(f32), axis=-1)
    stats = jnp.stack([log_norm * LOG2E, delta])
    lanes = group * T // D
    stats = stats.reshape(2, T, heads, group).transpose(2, 0, 3, 1).reshape(heads, 2 * lanes, D)
    stats = jnp.pad(stats, ((0, 0), (0, 8 - 2 * lanes), (0, 0)))
    stats = jnp.concatenate(pieces(stats), axis=1)
    stats = jnp.pad(stats, ((0, 0), (0, T - 24), (0, 0)))

    table = block_order.reshape(heads, inners, outers)

    def places(a, b):
        return lax.dynamic_slice(table, (0, a, b), (heads, 1, 1)).reshape(heads)

    keys_step, rows_step = 4, 2
    q_id, q_order = sort_down(places(i, o))
    me = lax.axis_index("head")
    before = (o - 1) % outers
    turn = jnp.where(o == 0, 1 - i, i)

    def order_of(*spots):
        k_id, k_order = sort_down(jnp.concatenate([places(a, b) for a, b in spots]))
        least = k_order.reshape(-1, keys_step * len(spots))[:, -1]
        seen = jnp.sum((q_order[None, :] >= least[:, None]).astype(jnp.int32), axis=1)
        return q_id, q_order, k_id, k_order, (seen + rows_step - 1) // rows_step

    tables = {
        "near": order_of((i, o)),
        "far_partner": order_of((1 - turn, before)),
        "others": order_of((1 - i, o), (turn, before)),
    }
    stats, tables = lax.optimization_barrier((stats, tables))
    packed = exchange(
        jnp.concatenate([by_head(query), by_head(grad_out), stats[:, None]], axis=1)
    )

    def part(name, contexts, dq, last, g_types):
        return attention_part(
            tables[name], packed, contexts, dq, last, keys_step * len(contexts), rows_step, g_types, name
        )

    def to_peers(blocks):
        return [blocks[0]] + [
            lax.ppermute(blocks[j], "head", [(h, h ^ j) for h in range(heads)])
            for j in range(1, heads)
        ]

    dq, near = part("near", [kv], None, False, [f32])
    dq, far_partner = part("far_partner", [kv_far_partner], dq, False, [bf16])
    far_partner = lax.ppermute(far_partner, ring, back)
    dq, near_partner, far = part("others", [kv_partner, kv_far], dq, True, [f32, bf16])
    partner = (near_partner + far_partner.astype(f32)).astype(bf16)
    partner, far = lax.optimization_barrier((partner, far))
    partner = lax.ppermute(partner, ring, swap)
    far = lax.ppermute(far, ring, back)
    dq = exchange(dq)
    grad = to_peers(add_by_peer(me, near, far, partner))
    dq = dq.reshape(q_heads, T, D).transpose(1, 0, 2)
    dq, grad = lax.optimization_barrier((dq, grad))
    return dq, *gather_grads(me, grad)


def solution(mesh):
    rows = P(("head", "inner", "outer"))
    return jax.shard_map(
        shards,
        mesh=mesh,
        in_specs=(rows,) * 6 + (P(),),
        out_specs=(rows,) * 3,
        check_vma=False,
    )
```

```python
import math

import jax
import jax.numpy as jnp
from jax import lax
from jax.experimental import pallas as pl
from jax.experimental.pallas import tpu as pltpu
from jax.sharding import PartitionSpec as P

LOG2E = math.log2(math.e)
NT = (((1,), (1,)), ((), ()))
NN = (((1,), (0,)), ((), ()))
f32 = jnp.float32
bf16 = jnp.bfloat16


def attention_part(
    tables, row, packed, contexts, dq_starts, last, keys_step, rows_step, heads, g_types, name
):
    src, _, T, D = contexts[0].shape
    R = heads * T
    many = len(contexts)
    n = many * src
    U, W = keys_step * T, rows_step * R
    groups = n // keys_step
    scale = D ** (-0.5)
    lanes = R // D

    def body(table, packed_ref, *rest):
        kv_refs, rest = rest[:many], rest[many:]
        start_refs, rest = rest[: len(dq_starts)], rest[len(dq_starts) :]
        out_ref, *rest = rest
        g_refs, rest = rest[:many], rest[many:]
        if many > 1:
            kv_s, g_s, *rest = rest
            for c in range(many):
                kv_s[c * src : (c + 1) * src] = kv_refs[c][...]
        else:
            kv_s, g_s = kv_refs[0], g_refs[0]
        st_s, k_s, v_s, kt_s, dk_s, dv_s, *rest = rest
        dq_s = rest[0] if last else out_ref
        dq_s[...] = sum((r[...] for r in start_refs), jnp.zeros_like(dq_s))
        kid = lambda j: table[row, j]
        kord = lambda j: table[row + 1, j]

        def prepare(i, carry):
            st = packed_ref[table[0, i], 2 * R :].astype(f32)
            st = st[0:8] + st[8:16] + st[16:24]
            st_s[i, 0:1] = jnp.concatenate([st[j : j + 1] for j in range(lanes)], axis=1)
            st_s[i, 1:2] = jnp.concatenate([st[j : j + 1] for j in range(lanes, 2 * lanes)], axis=1)
            return carry

        lax.fori_loop(0, src, prepare, 0)
        lead = lax.broadcasted_iota(jnp.int32, (T, R), 1) % T - lax.broadcasted_iota(
            jnp.int32, (T, R), 0
        )

        def group(g, carry):
            for j in range(keys_step):
                b = kid(g * keys_step + j)
                k_s[pl.ds(j * T, T)] = kv_s[b, 0]
                v_s[pl.ds(j * T, T)] = kv_s[b, 1]
            kt_s[...] = k_s[...].T
            dk_s[...] = jnp.zeros_like(dk_s)
            dv_s[...] = jnp.zeros_like(dv_s)

            def step(i, inner):
                at = pl.ds(pl.multiple_of(i * W, W), W)
                ids = [table[0, i * rows_step + h] for h in range(rows_step)]
                q = jnp.concatenate([packed_ref[b, 0:R] for b in ids], axis=0)
                do = jnp.concatenate([packed_ref[b, R : 2 * R] for b in ids], axis=0)
                k, v = k_s[...], v_s[...]
                s = lax.dot_general(k, q, NT, preferred_element_type=f32)
                dp = lax.dot_general(v, do, NT, preferred_element_type=f32)
                p_cols, ds_cols = [], []
                for h in range(rows_step):
                    at_row = i * rows_step + h
                    lse, delta, place = st_s[at_row, 0:1], st_s[at_row, 1:2], table[1, at_row]
                    p_rows, ds_rows = [], []
                    for j in range(keys_step):
                        behind = (kord(g * keys_step + j) - place) * T
                        cut = (slice(j * T, (j + 1) * T), slice(h * R, (h + 1) * R))
                        p = jnp.where(
                            lead >= behind, jnp.exp2(s[cut] * (scale * LOG2E) - lse), 0.0
                        )
                        ds_rows.append((p * (dp[cut] - delta)).astype(bf16))
                        p_rows.append(p.astype(bf16))
                    p_cols.append(jnp.concatenate(p_rows, axis=0))
                    ds_cols.append(jnp.concatenate(ds_rows, axis=0))
                p, ds = jnp.concatenate(p_cols, axis=1), jnp.concatenate(ds_cols, axis=1)
                dv_s[...] += lax.dot_general(p, do, NN, preferred_element_type=f32)
                dk_s[...] += lax.dot_general(ds, q, NN, preferred_element_type=f32)
                dq_s[:, at] += lax.dot_general(kt_s[...], ds, NN, preferred_element_type=f32)
                return inner

            steps = (table[row + 2, g] + rows_step - 1) // rows_step
            lax.fori_loop(0, steps, step, 0)
            for j in range(keys_step):
                b = kid(g * keys_step + j)
                g_s[b, 0] = (dk_s[pl.ds(j * T, T)] * scale).astype(g_s.dtype)
                g_s[b, 1] = dv_s[pl.ds(j * T, T)].astype(g_s.dtype)
            return carry

        lax.fori_loop(0, groups, group, 0)
        if many > 1:
            for c in range(many):
                g_refs[c][...] = g_s[c * src : (c + 1) * src].astype(g_refs[c].dtype)
        if last:
            for j in range(src):
                at = pl.ds(j * R, R)
                out_ref[table[0, j]] = (dq_s[:, at].T * scale).astype(bf16).reshape(heads, T, D)

    smem = pl.BlockSpec(memory_space=pltpu.SMEM)
    vmem = pl.BlockSpec(memory_space=pltpu.VMEM)
    if last:
        dq_out = jax.ShapeDtypeStruct((src, heads, T, D), bf16)
    else:
        dq_out = jax.ShapeDtypeStruct((D, src * R), f32)
    g_outs = [jax.ShapeDtypeStruct((src, 2, T, D), t) for t in g_types]
    scratch = []
    if many > 1:
        scratch = [pltpu.VMEM((n, 2, T, D), bf16), pltpu.VMEM((n, 2, T, D), f32)]
    scratch += [
        pltpu.VMEM((src, 8, R), f32),
        pltpu.VMEM((U, D), bf16),
        pltpu.VMEM((U, D), bf16),
        pltpu.VMEM((D, U), bf16),
        pltpu.VMEM((U, D), f32),
        pltpu.VMEM((U, D), f32),
    ]
    if last:
        scratch.append(pltpu.VMEM((D, src * R), f32))
    arrays = [packed, *contexts, *dq_starts]
    return pl.pallas_call(
        body,
        out_shape=(dq_out, *g_outs),
        in_specs=[smem] + [vmem] * len(arrays),
        out_specs=(vmem,) * (1 + many),
        scratch_shapes=scratch,
        compiler_params=pltpu.CompilerParams(vmem_limit_bytes=32 * 2**20),
        cost_estimate=pl.CostEstimate(flops=1, bytes_accessed=1, transcendentals=0),
        name=name,
    )(tables, *arrays)


def add_by_peer(*arrays):
    src, *rest = arrays[0].shape

    def body(*refs):
        ins, outs = refs[: len(arrays)], refs[len(arrays) :]
        me = lax.axis_index("head")
        for j in range(src):
            at = me ^ j
            outs[j][...] = sum(r[at].astype(f32) for r in ins).astype(bf16)

    vmem = pl.BlockSpec(memory_space=pltpu.VMEM)
    return pl.pallas_call(
        body,
        out_shape=[jax.ShapeDtypeStruct(rest, bf16)] * src,
        in_specs=[vmem] * len(arrays),
        out_specs=[vmem] * src,
        cost_estimate=pl.CostEstimate(flops=10**10, bytes_accessed=1, transcendentals=0),
        name="add_by_peer",
    )(*arrays)


def gather_grads(pieces):
    src = len(pieces)
    _, T, D = pieces[0].shape

    def body(*refs):
        me = lax.axis_index("head")
        ins, outs, held, wide = refs[:src], refs[src : src + 2], refs[-2], refs[-1]
        for j in range(src):
            held[me ^ j] = ins[j][...]
        for c in range(2):
            for g in range(src):
                wide[:, g, :] = held[g, c].astype(f32)
            outs[c][...] = wide[...].astype(bf16)

    vmem = pl.BlockSpec(memory_space=pltpu.VMEM)
    return pl.pallas_call(
        body,
        out_shape=[jax.ShapeDtypeStruct((T, src, D), bf16)] * 2,
        in_specs=[vmem] * src,
        out_specs=[vmem] * 2,
        scratch_shapes=[pltpu.VMEM((src, 2, T, D), bf16), pltpu.VMEM((T, src, D), f32)],
        name="gather_grads",
    )(*pieces)


def order_tables(block_order, spots_of, heads, inners, outers, keys_step):
    wide = 128

    def body(order_ref, out_ref):
        table = order_ref[...]
        sub = lax.broadcasted_iota(jnp.int32, table.shape, 0)
        spot = lax.broadcasted_iota(jnp.int32, table.shape, 1)

        def sort(spots):
            n = heads * len(spots)
            down = jnp.concatenate(
                [
                    jnp.sum(jnp.where(spot == a * outers + b, table, 0), axis=1, keepdims=True)
                    for a, b in spots
                ],
                axis=0,
            )
            s = lax.broadcasted_iota(jnp.int32, (n, wide), 0)
            lane = lax.broadcasted_iota(jnp.int32, (n, wide), 1)
            across = jnp.sum(jnp.where(s == lane, down, 0), axis=0, keepdims=True)
            ahead = jnp.where((across > down) & (lane < n), 1, 0)
            hit = jnp.sum(ahead, axis=1, keepdims=True) == lane
            ids = jnp.sum(jnp.where(hit, s, 0), axis=0, keepdims=True)
            return ids, jnp.sum(jnp.where(hit, down, 0), axis=0, keepdims=True)

        own, lists = spots_of()
        q_id, q_order = sort([own])
        rows = [q_id, q_order]
        lane = lax.broadcasted_iota(jnp.int32, (1, wide), 1)
        for spots in lists:
            ids, order = sort(spots)
            step = keys_step * len(spots)
            seen = jnp.zeros((1, wide), jnp.int32)
            for g in range(heads * len(spots) // step):
                least = jnp.sum(
                    jnp.where(lane == (g + 1) * step - 1, order, 0), axis=1, keepdims=True
                )
                count = jnp.sum(
                    jnp.where((q_order >= least) & (lane < heads), 1, 0), axis=1, keepdims=True
                )
                seen = jnp.where(lane == g, count, seen)
            rows += [ids, order, seen]
        rows.append(jnp.zeros((16 - len(rows), wide), jnp.int32))
        out_ref[...] = jnp.concatenate(rows, axis=0)

    vmem = pl.BlockSpec(memory_space=pltpu.VMEM)
    return pl.pallas_call(
        body,
        out_shape=jax.ShapeDtypeStruct((16, wide), jnp.int32),
        in_specs=[vmem],
        out_specs=vmem,
        name="order_tables",
    )(block_order.reshape(heads, inners * outers))


def pieces(x):
    high = lax.reduce_precision(x, 8, 7)
    rest = x - high
    middle = lax.reduce_precision(rest, 8, 7)
    return [v.astype(bf16) for v in (high, middle, rest - middle)]


def shards(query, keys, values, attn_out, grad_out, log_norm, block_order):
    heads = lax.axis_size("head")
    inners = lax.axis_size("inner")
    outers = lax.axis_size("outer")
    T, q_heads, D = query.shape
    group = q_heads // keys.shape[1]

    ring = ("inner", "outer")
    place = lambda a, b: a * outers + b
    swap = [(place(1 - a, b), place(a, b)) for a in range(inners) for b in range(outers)]
    ahead = [
        (place(a, b), place(a, b + 1) if b + 1 < outers else place(1 - a, 0))
        for a in range(inners)
        for b in range(outers)
    ]
    across = [(dict(swap)[a], b) for a, b in ahead]
    back = [(b, a) for a, b in ahead]

    def exchange(x):
        return lax.all_to_all(x, "head", split_axis=0, concat_axis=0, tiled=True)

    def by_head(x):
        return x.reshape(T, heads, -1, D).transpose(1, 2, 0, 3)

    kv = exchange(jnp.concatenate([by_head(keys), by_head(values)], axis=1))
    kv_far_partner = lax.ppermute(kv, ring, across)
    kv_far = lax.ppermute(kv, ring, ahead)
    kv_after, kv_far_partner = lax.optimization_barrier((kv, kv_far_partner))
    kv_partner = lax.ppermute(kv_after, ring, swap)

    delta = jnp.sum(grad_out.astype(f32) * attn_out.astype(f32), axis=-1)
    stats = jnp.stack([log_norm * LOG2E, delta])
    lanes = group * T // D
    stats = stats.reshape(2, T, heads, group).transpose(2, 0, 3, 1).reshape(heads, 2 * lanes, D)
    stats = jnp.pad(stats, ((0, 0), (0, 8 - 2 * lanes), (0, 0)))
    stats = jnp.concatenate(pieces(stats), axis=1)
    stats = jnp.pad(stats, ((0, 0), (0, 8), (0, 0)))
    keys_step, rows_step = 4, 2
    names = ["far_partner", "far", "near_partner", "near"]

    def spots_of():
        a, b = lax.axis_index("inner"), lax.axis_index("outer")
        before = jnp.where(b == 0, outers - 1, b - 1)
        turn = jnp.where(b == 0, 1 - a, a)
        lists = [[(1 - turn, before)], [(turn, before)], [(1 - a, b)], [(a, b)]]
        return (a, b), lists

    tables = order_tables(block_order, spots_of, heads, inners, outers, keys_step)
    rows_of = lambda x: by_head(x).reshape(heads, group * T, D)
    stats, tables = lax.optimization_barrier((stats, tables))
    packed = exchange(jnp.concatenate([rows_of(query), rows_of(grad_out), stats], axis=1))
    def part(name, contexts, dq_starts, last, g_types):
        return attention_part(
            tables,
            2 + 3 * names.index(name),
            packed,
            contexts,
            dq_starts,
            last,
            keys_step * len(contexts),
            rows_step,
            group,
            g_types,
            name,
        )

    def to_peers(blocks):
        return [blocks[0]] + [
            lax.ppermute(blocks[j], "head", [(h, h ^ j) for h in range(heads)])
            for j in range(1, heads)
        ]

    dq, far_partner = part("far_partner", [kv_far_partner], [], False, [bf16])
    far_partner = lax.ppermute(far_partner, ring, back)
    starts = [dq]
    packed, dq = lax.optimization_barrier((packed, dq))
    dq, far = part("far", [kv_far], [], False, [bf16])
    far = lax.ppermute(far, ring, back)
    starts.append(dq)
    packed, dq = lax.optimization_barrier((packed, dq))
    dq, near_partner = part("near_partner", [kv_partner], starts, False, [f32])
    partner = (near_partner + far_partner.astype(f32)).astype(bf16)
    partner = lax.ppermute(partner, ring, swap)
    dq, near = part("near", [kv], [dq], True, [f32])
    dq = exchange(dq)
    grad = to_peers(add_by_peer(near, partner, far))
    dq = dq.reshape(q_heads, T, D).transpose(1, 0, 2)
    dq, grad = lax.optimization_barrier((dq, grad))
    return dq, *gather_grads(grad)


def solution(mesh):
    rows = P(("head", "inner", "outer"))
    return jax.shard_map(
        shards,
        mesh=mesh,
        in_specs=(rows,) * 6 + (P(),),
        out_specs=(rows,) * 3,
        check_vma=False,
    )
```

```python
import math

import jax
import jax.numpy as jnp
from jax import lax
from jax.experimental import pallas as pl
from jax.experimental.pallas import tpu as pltpu
from jax.sharding import PartitionSpec as P

LOG2E = math.log2(math.e)
NT = (((1,), (1,)), ((), ()))
NN = (((1,), (0,)), ((), ()))
PARAMS = pltpu.CompilerParams(vmem_limit_bytes=32 * 2**20)
f32 = jnp.float32
bf16 = jnp.bfloat16


def attention_part(
    tables, row, packed, contexts, dq_starts, last, keys_step, rows_step, heads, g_types, name
):
    src, _, T, D = contexts[0].shape
    R = heads * T
    many = len(contexts)
    n = many * src
    U, W = keys_step * T, rows_step * R
    groups = n // keys_step
    scale = D ** (-0.5)
    lanes = R // D

    def body(table, packed_ref, *rest):
        kv_refs, rest = rest[:many], rest[many:]
        start_refs, rest = rest[: len(dq_starts)], rest[len(dq_starts) :]
        out_ref, *rest = rest
        g_refs, rest = rest[:many], rest[many:]
        if many > 1:
            kv_s, g_s, *rest = rest
            for c in range(many):
                kv_s[c * src : (c + 1) * src] = kv_refs[c][...]
        else:
            kv_s, g_s = kv_refs[0], g_refs[0]
        st_s, k_s, v_s, kt_s, dk_s, dv_s, *rest = rest
        dq_s = rest[0] if last else out_ref
        dq_s[...] = sum((r[...] for r in start_refs), jnp.zeros_like(dq_s))
        kid = lambda j: table[row, j]
        kord = lambda j: table[row + 1, j]

        def prepare(i, carry):
            st = packed_ref[table[0, i], 2 * R :].astype(f32)
            st = st[0:8] + st[8:16] + st[16:24]
            st_s[i, 0:1] = jnp.concatenate([st[j : j + 1] for j in range(lanes)], axis=1)
            st_s[i, 1:2] = jnp.concatenate([st[j : j + 1] for j in range(lanes, 2 * lanes)], axis=1)
            return carry

        lax.fori_loop(0, src, prepare, 0)
        lead = lax.broadcasted_iota(jnp.int32, (T, R), 1) % T - lax.broadcasted_iota(
            jnp.int32, (T, R), 0
        )

        def group(g, carry):
            for j in range(keys_step):
                b = kid(g * keys_step + j)
                k_s[pl.ds(j * T, T)] = kv_s[b, 0]
                v_s[pl.ds(j * T, T)] = kv_s[b, 1]
            kt_s[...] = k_s[...].T
            dk_s[...] = jnp.zeros_like(dk_s)
            dv_s[...] = jnp.zeros_like(dv_s)

            def step(i, inner):
                at = pl.ds(pl.multiple_of(i * W, W), W)
                ids = [table[0, i * rows_step + h] for h in range(rows_step)]
                q = jnp.concatenate([packed_ref[b, 0:R] for b in ids], axis=0)
                do = jnp.concatenate([packed_ref[b, R : 2 * R] for b in ids], axis=0)
                k, v = k_s[...], v_s[...]
                s = lax.dot_general(k, q, NT, preferred_element_type=f32)
                dp = lax.dot_general(v, do, NT, preferred_element_type=f32)
                p_cols, ds_cols = [], []
                for h in range(rows_step):
                    at_row = i * rows_step + h
                    lse, delta, place = st_s[at_row, 0:1], st_s[at_row, 1:2], table[1, at_row]
                    p_rows, ds_rows = [], []
                    for j in range(keys_step):
                        behind = (kord(g * keys_step + j) - place) * T
                        cut = (slice(j * T, (j + 1) * T), slice(h * R, (h + 1) * R))
                        p = jnp.where(
                            lead >= behind, jnp.exp2(s[cut] * (scale * LOG2E) - lse), 0.0
                        )
                        ds_rows.append((p * (dp[cut] - delta)).astype(bf16))
                        p_rows.append(p.astype(bf16))
                    p_cols.append(jnp.concatenate(p_rows, axis=0))
                    ds_cols.append(jnp.concatenate(ds_rows, axis=0))
                p, ds = jnp.concatenate(p_cols, axis=1), jnp.concatenate(ds_cols, axis=1)
                dv_s[...] += lax.dot_general(p, do, NN, preferred_element_type=f32)
                dk_s[...] += lax.dot_general(ds, q, NN, preferred_element_type=f32)
                dq_s[:, at] += lax.dot_general(kt_s[...], ds, NN, preferred_element_type=f32)
                return inner

            steps = (table[row + 2, g] + rows_step - 1) // rows_step
            lax.fori_loop(0, steps, step, 0)
            for j in range(keys_step):
                b = kid(g * keys_step + j)
                g_s[b, 0] = (dk_s[pl.ds(j * T, T)] * scale).astype(g_s.dtype)
                g_s[b, 1] = dv_s[pl.ds(j * T, T)].astype(g_s.dtype)
            return carry

        lax.fori_loop(0, groups, group, 0)
        if many > 1:
            for c in range(many):
                g_refs[c][...] = g_s[c * src : (c + 1) * src].astype(g_refs[c].dtype)
        if last:
            stage, sems = rest[1:]
            copies = []
            for j in range(src):
                stage[j] = (dq_s[:, j * R : (j + 1) * R].T * scale).astype(bf16)
                copies.append(
                    pltpu.make_async_copy(stage.at[j], out_ref.at[table[0, j]], sems.at[j])
                )
                copies[-1].start()
            for copy in copies:
                copy.wait()

    smem = pl.BlockSpec(memory_space=pltpu.SMEM)
    vmem = pl.BlockSpec(memory_space=pltpu.VMEM)
    if last:
        dq_out = jax.ShapeDtypeStruct((src, R, D), bf16)
    else:
        dq_out = jax.ShapeDtypeStruct((D, src * R), f32)
    g_outs = [jax.ShapeDtypeStruct((src, 2, T, D), t) for t in g_types]
    scratch = []
    if many > 1:
        scratch = [pltpu.VMEM((n, 2, T, D), bf16), pltpu.VMEM((n, 2, T, D), f32)]
    scratch += [
        pltpu.VMEM((src, 8, R), f32),
        pltpu.VMEM((U, D), bf16),
        pltpu.VMEM((U, D), bf16),
        pltpu.VMEM((D, U), bf16),
        pltpu.VMEM((U, D), f32),
        pltpu.VMEM((U, D), f32),
    ]
    if last:
        scratch += [
            pltpu.VMEM((D, src * R), f32),
            pltpu.VMEM((src, R, D), bf16),
            pltpu.SemaphoreType.DMA((src,)),
        ]
    arrays = [packed, *contexts, *dq_starts]
    return pl.pallas_call(
        body,
        out_shape=(dq_out, *g_outs),
        in_specs=[smem] + [vmem] * len(arrays),
        out_specs=(pl.BlockSpec(memory_space=pltpu.HBM) if last else vmem,) + (vmem,) * many,
        scratch_shapes=scratch,
        compiler_params=PARAMS,
        cost_estimate=pl.CostEstimate(flops=1, bytes_accessed=1, transcendentals=0),
        name=name,
    )(tables, *arrays)


def add_by_peer(*arrays):
    src, *rest = arrays[0].shape

    def body(*refs):
        ins, outs = refs[: len(arrays)], refs[len(arrays) :]
        me = lax.axis_index("head")
        for j in range(src):
            at = me ^ j
            outs[j][...] = sum(r[at].astype(f32) for r in ins).astype(bf16)

    vmem = pl.BlockSpec(memory_space=pltpu.VMEM)
    return pl.pallas_call(
        body,
        out_shape=[jax.ShapeDtypeStruct(rest, bf16)] * src,
        in_specs=[vmem] * len(arrays),
        out_specs=[vmem] * src,
        cost_estimate=pl.CostEstimate(flops=10**10, bytes_accessed=1, transcendentals=0),
        compiler_params=PARAMS,
        name="add_by_peer",
    )(*arrays)


def gather_grads(pieces):
    src = len(pieces)
    _, T, D = pieces[0].shape

    def body(*refs):
        me = lax.axis_index("head")
        ins, outs, held, wide = refs[:src], refs[src : src + 2], refs[-2], refs[-1]
        for j in range(src):
            held[me ^ j] = ins[j][...]
        for c in range(2):
            for g in range(src):
                wide[:, g, :] = held[g, c].astype(f32)
            outs[c][...] = wide[...].astype(bf16)

    vmem = pl.BlockSpec(memory_space=pltpu.VMEM)
    return pl.pallas_call(
        body,
        out_shape=[jax.ShapeDtypeStruct((T, src, D), bf16)] * 2,
        in_specs=[vmem] * src,
        out_specs=[vmem] * 2,
        scratch_shapes=[pltpu.VMEM((src, 2, T, D), bf16), pltpu.VMEM((T, src, D), f32)],
        compiler_params=PARAMS,
        name="gather_grads",
    )(*pieces)


def order_tables(block_order, spots_of, heads, inners, outers, keys_step):
    wide = 128

    def body(order_ref, out_ref):
        def sort(spots):
            n = heads * len(spots)
            s = lax.broadcasted_iota(jnp.int32, (n, wide), 0)
            lane = lax.broadcasted_iota(jnp.int32, (n, wide), 1)
            down, across = jnp.zeros_like(s), jnp.zeros_like(s)
            for c, (a, b) in enumerate(spots):
                for h in range(heads):
                    place = order_ref[(h * inners + a) * outers + b]
                    down = jnp.where(s == c * heads + h, place, down)
                    across = jnp.where(lane == c * heads + h, place, across)
            ahead = jnp.where((across > down) & (lane < n), 1, 0)
            hit = jnp.sum(ahead, axis=1, keepdims=True) == lane
            ids = jnp.sum(jnp.where(hit, s, 0), axis=0, keepdims=True)
            return ids, jnp.sum(jnp.where(hit, down, 0), axis=0, keepdims=True)

        own, lists = spots_of()
        q_id, q_order = sort([own])
        rows = [q_id, q_order]
        lane = lax.broadcasted_iota(jnp.int32, (1, wide), 1)
        for spots in lists:
            ids, order = sort(spots)
            step = keys_step * len(spots)
            seen = jnp.zeros((1, wide), jnp.int32)
            for g in range(heads * len(spots) // step):
                least = jnp.sum(
                    jnp.where(lane == (g + 1) * step - 1, order, 0), axis=1, keepdims=True
                )
                count = jnp.sum(
                    jnp.where((q_order >= least) & (lane < heads), 1, 0), axis=1, keepdims=True
                )
                seen = jnp.where(lane == g, count, seen)
            rows += [ids, order, seen]
        rows.append(jnp.zeros((16 - len(rows), wide), jnp.int32))
        out_ref[...] = jnp.concatenate(rows, axis=0)

    return pl.pallas_call(
        body,
        out_shape=jax.ShapeDtypeStruct((16, wide), jnp.int32),
        in_specs=[pl.BlockSpec(memory_space=pltpu.SMEM)],
        out_specs=pl.BlockSpec(memory_space=pltpu.VMEM),
        compiler_params=PARAMS,
        name="order_tables",
    )(block_order)


def pieces(x):
    high = lax.reduce_precision(x, 8, 7)
    rest = x - high
    middle = lax.reduce_precision(rest, 8, 7)
    return [v.astype(bf16) for v in (high, middle, rest - middle)]


def shards(query, keys, values, attn_out, grad_out, log_norm, block_order):
    heads = lax.axis_size("head")
    inners = lax.axis_size("inner")
    outers = lax.axis_size("outer")
    T, q_heads, D = query.shape
    group = q_heads // keys.shape[1]

    ring = ("inner", "outer")
    place = lambda a, b: a * outers + b
    swap = [(place(1 - a, b), place(a, b)) for a in range(inners) for b in range(outers)]
    ahead = [
        (place(a, b), place(a, b + 1) if b + 1 < outers else place(1 - a, 0))
        for a in range(inners)
        for b in range(outers)
    ]
    across = [(dict(swap)[a], b) for a, b in ahead]
    back = [(b, a) for a, b in ahead]

    def exchange(x):
        return lax.all_to_all(x, "head", split_axis=0, concat_axis=0, tiled=True)

    def by_head(x):
        return x.reshape(T, heads, -1, D).transpose(1, 2, 0, 3)

    kv = exchange(jnp.concatenate([by_head(keys), by_head(values)], axis=1))
    kv_far_partner = lax.ppermute(kv, ring, across)
    kv_far = lax.ppermute(kv, ring, ahead)
    kv_after, kv_far_partner = lax.optimization_barrier((kv, kv_far_partner))
    kv_partner = lax.ppermute(kv_after, ring, swap)

    delta = jnp.sum(grad_out.astype(f32) * attn_out.astype(f32), axis=-1)
    stats = jnp.stack([log_norm * LOG2E, delta])
    lanes = group * T // D
    stats = stats.reshape(2, T, heads, group).transpose(2, 0, 3, 1).reshape(heads, 2 * lanes, D)
    stats = jnp.pad(stats, ((0, 0), (0, 8 - 2 * lanes), (0, 0)))
    stats = jnp.concatenate(pieces(stats), axis=1)
    stats = jnp.pad(stats, ((0, 0), (0, 8), (0, 0)))
    keys_step, rows_step = 4, 2
    names = ["far_partner", "far", "near_partner", "near"]

    def spots_of():
        a, b = lax.axis_index("inner"), lax.axis_index("outer")
        before = jnp.where(b == 0, outers - 1, b - 1)
        turn = jnp.where(b == 0, 1 - a, a)
        lists = [[(1 - turn, before)], [(turn, before)], [(1 - a, b)], [(a, b)]]
        return (a, b), lists

    tables = order_tables(block_order, spots_of, heads, inners, outers, keys_step)
    rows_of = lambda x: by_head(x).reshape(heads, group * T, D)
    stats, tables = lax.optimization_barrier((stats, tables))
    packed = exchange(jnp.concatenate([rows_of(query), rows_of(grad_out), stats], axis=1))
    def part(name, contexts, dq_starts, last, g_types):
        return attention_part(
            tables,
            2 + 3 * names.index(name),
            packed,
            contexts,
            dq_starts,
            last,
            keys_step * len(contexts),
            rows_step,
            group,
            g_types,
            name,
        )

    def to_peers(blocks):
        return [blocks[0]] + [
            lax.ppermute(blocks[j], "head", [(h, h ^ j) for h in range(heads)])
            for j in range(1, heads)
        ]

    dq, far_partner = part("far_partner", [kv_far_partner], [], False, [bf16])
    far_partner = lax.ppermute(far_partner, ring, back)
    starts = [dq]
    packed, dq = lax.optimization_barrier((packed, dq))
    dq, far = part("far", [kv_far], [], False, [bf16])
    far = lax.ppermute(far, ring, back)
    starts.append(dq)
    packed, dq = lax.optimization_barrier((packed, dq))
    dq, near_partner = part("near_partner", [kv_partner], starts, False, [f32])
    partner = (near_partner + far_partner.astype(f32)).astype(bf16)
    partner = lax.ppermute(partner, ring, swap)
    dq, near = part("near", [kv], [dq], True, [f32])
    dq = exchange(dq)
    grad = to_peers(add_by_peer(near, partner, far))
    dq = dq.reshape(q_heads, T, D).transpose(1, 0, 2)
    dq, grad = lax.optimization_barrier((dq, grad))
    return dq, *gather_grads(grad)


def solution(mesh):
    rows = P(("head", "inner", "outer"))
    return jax.shard_map(
        shards,
        mesh=mesh,
        in_specs=(rows,) * 6 + (P(),),
        out_specs=(rows,) * 3,
        check_vma=False,
    )
```

```python
import math

import jax
import jax.numpy as jnp
from jax import lax
from jax.experimental import pallas as pl
from jax.experimental.pallas import tpu as pltpu
from jax.sharding import PartitionSpec as P

LOG2E = math.log2(math.e)
NT = (((1,), (1,)), ((), ()))
NN = (((1,), (0,)), ((), ()))
PARAMS = pltpu.CompilerParams(vmem_limit_bytes=32 * 2**20)
f32 = jnp.float32
bf16 = jnp.bfloat16


def attention_part(
    tables, row, packed, contexts, dq_starts, last, keys_step, rows_step, heads, g_types, name
):
    src, _, T, D = contexts[0].shape
    R = heads * T
    many = len(contexts)
    n = many * src
    U, W = keys_step * T, rows_step * R
    groups = n // keys_step
    scale = D ** (-0.5)
    lanes = R // D

    def body(table, packed_ref, *rest):
        kv_refs, rest = rest[:many], rest[many:]
        start_refs, rest = rest[: len(dq_starts)], rest[len(dq_starts) :]
        out_ref, *rest = rest
        g_refs, rest = rest[:many], rest[many:]
        if many > 1:
            kv_s, g_s, *rest = rest
            for c in range(many):
                kv_s[c * src : (c + 1) * src] = kv_refs[c][...]
        else:
            kv_s, g_s = kv_refs[0], g_refs[0]
        st_s, k_s, v_s, kt_s, dk_s, dv_s, *rest = rest
        dq_s = rest[0] if last else out_ref
        dq_s[...] = sum((r[...] for r in start_refs), jnp.zeros_like(dq_s))
        kid = lambda j: table[row, j]
        kord = lambda j: table[row + 1, j]

        def prepare(i, carry):
            st = packed_ref[table[0, i], 2 * R :].astype(f32)
            st = st[0:8] + st[8:16] + st[16:24]
            st_s[i, 0:1] = jnp.concatenate([st[j : j + 1] for j in range(lanes)], axis=1)
            st_s[i, 1:2] = jnp.concatenate([st[j : j + 1] for j in range(lanes, 2 * lanes)], axis=1)
            return carry

        lax.fori_loop(0, src, prepare, 0)
        lead = lax.broadcasted_iota(jnp.int32, (T, R), 1) % T - lax.broadcasted_iota(
            jnp.int32, (T, R), 0
        )

        def group(g, carry):
            for j in range(keys_step):
                b = kid(g * keys_step + j)
                k_s[pl.ds(j * T, T)] = kv_s[b, 0]
                v_s[pl.ds(j * T, T)] = kv_s[b, 1]
            kt_s[...] = k_s[...].T
            dk_s[...] = jnp.zeros_like(dk_s)
            dv_s[...] = jnp.zeros_like(dv_s)

            def step(i, inner):
                at = pl.ds(pl.multiple_of(i * W, W), W)
                ids = [table[0, i * rows_step + h] for h in range(rows_step)]
                q = jnp.concatenate([packed_ref[b, 0:R] for b in ids], axis=0)
                do = jnp.concatenate([packed_ref[b, R : 2 * R] for b in ids], axis=0)
                k, v = k_s[...], v_s[...]
                s = lax.dot_general(k, q, NT, preferred_element_type=f32)
                dp = lax.dot_general(v, do, NT, preferred_element_type=f32)
                p_cols, ds_cols = [], []
                for h in range(rows_step):
                    at_row = i * rows_step + h
                    lse, delta, place = st_s[at_row, 0:1], st_s[at_row, 1:2], table[1, at_row]
                    p_rows, ds_rows = [], []
                    for j in range(keys_step):
                        behind = (kord(g * keys_step + j) - place) * T
                        cut = (slice(j * T, (j + 1) * T), slice(h * R, (h + 1) * R))
                        p = jnp.where(
                            lead >= behind, jnp.exp2(s[cut] * (scale * LOG2E) - lse), 0.0
                        )
                        ds_rows.append((p * (dp[cut] - delta)).astype(bf16))
                        p_rows.append(p.astype(bf16))
                    p_cols.append(jnp.concatenate(p_rows, axis=0))
                    ds_cols.append(jnp.concatenate(ds_rows, axis=0))
                p, ds = jnp.concatenate(p_cols, axis=1), jnp.concatenate(ds_cols, axis=1)
                dv_s[...] += lax.dot_general(p, do, NN, preferred_element_type=f32)
                dk_s[...] += lax.dot_general(ds, q, NN, preferred_element_type=f32)
                dq_s[:, at] += lax.dot_general(kt_s[...], ds, NN, preferred_element_type=f32)
                return inner

            steps = (table[row + 2, g] + rows_step - 1) // rows_step
            lax.fori_loop(0, steps, step, 0)
            for j in range(keys_step):
                b = kid(g * keys_step + j)
                g_s[b, 0] = (dk_s[pl.ds(j * T, T)] * scale).astype(g_s.dtype)
                g_s[b, 1] = dv_s[pl.ds(j * T, T)].astype(g_s.dtype)
            return carry

        lax.fori_loop(0, groups, group, 0)
        if many > 1:
            for c in range(many):
                g_refs[c][...] = g_s[c * src : (c + 1) * src].astype(g_refs[c].dtype)
        if last:
            stage, sems = rest[1:]
            copies = []
            for j in range(src):
                stage[j] = (dq_s[:, j * R : (j + 1) * R] * scale).astype(bf16).T
                copies.append(
                    pltpu.make_async_copy(stage.at[j], out_ref.at[table[0, j]], sems.at[j])
                )
                copies[-1].start()
            for copy in copies:
                copy.wait()

    smem = pl.BlockSpec(memory_space=pltpu.SMEM)
    vmem = pl.BlockSpec(memory_space=pltpu.VMEM)
    if last:
        dq_out = jax.ShapeDtypeStruct((src, R, D), bf16)
    else:
        dq_out = jax.ShapeDtypeStruct((D, src * R), f32)
    g_outs = [jax.ShapeDtypeStruct((src, 2, T, D), t) for t in g_types]
    scratch = []
    if many > 1:
        scratch = [pltpu.VMEM((n, 2, T, D), bf16), pltpu.VMEM((n, 2, T, D), f32)]
    scratch += [
        pltpu.VMEM((src, 8, R), f32),
        pltpu.VMEM((U, D), bf16),
        pltpu.VMEM((U, D), bf16),
        pltpu.VMEM((D, U), bf16),
        pltpu.VMEM((U, D), f32),
        pltpu.VMEM((U, D), f32),
    ]
    if last:
        scratch += [
            pltpu.VMEM((D, src * R), f32),
            pltpu.VMEM((src, R, D), bf16),
            pltpu.SemaphoreType.DMA((src,)),
        ]
    arrays = [packed, *contexts, *dq_starts]
    return pl.pallas_call(
        body,
        out_shape=(dq_out, *g_outs),
        in_specs=[smem] + [vmem] * len(arrays),
        out_specs=(pl.BlockSpec(memory_space=pltpu.HBM) if last else vmem,) + (vmem,) * many,
        scratch_shapes=scratch,
        compiler_params=PARAMS,
        cost_estimate=pl.CostEstimate(flops=1, bytes_accessed=1, transcendentals=0),
        name=name,
    )(tables, *arrays)


def add_by_peer(*arrays):
    src, *rest = arrays[0].shape

    def body(*refs):
        ins, outs = refs[: len(arrays)], refs[len(arrays) :]
        me = lax.axis_index("head")
        for j in range(src):
            at = me ^ j
            outs[j][...] = sum(r[at].astype(f32) for r in ins).astype(bf16)

    vmem = pl.BlockSpec(memory_space=pltpu.VMEM)
    return pl.pallas_call(
        body,
        out_shape=[jax.ShapeDtypeStruct(rest, bf16)] * src,
        in_specs=[vmem] * len(arrays),
        out_specs=[vmem] * src,
        cost_estimate=pl.CostEstimate(flops=10**10, bytes_accessed=1, transcendentals=0),
        compiler_params=PARAMS,
        name="add_by_peer",
    )(*arrays)


def gather_grads(pieces):
    src = len(pieces)
    _, T, D = pieces[0].shape

    def body(*refs):
        me = lax.axis_index("head")
        ins, outs, held, wide = refs[:src], refs[src : src + 2], refs[-2], refs[-1]
        for j in range(src):
            held[me ^ j] = ins[j][...]
        for c in range(2):
            for g in range(src):
                wide[:, g, :] = held[g, c].astype(f32)
            outs[c][...] = wide[...].astype(bf16)

    vmem = pl.BlockSpec(memory_space=pltpu.VMEM)
    return pl.pallas_call(
        body,
        out_shape=[jax.ShapeDtypeStruct((T, src, D), bf16)] * 2,
        in_specs=[vmem] * src,
        out_specs=[vmem] * 2,
        scratch_shapes=[pltpu.VMEM((src, 2, T, D), bf16), pltpu.VMEM((T, src, D), f32)],
        compiler_params=PARAMS,
        name="gather_grads",
    )(*pieces)


def order_tables(block_order, spots_of, heads, inners, outers, keys_step):
    wide = 128

    def body(order_ref, out_ref):
        def sort(spots):
            n = heads * len(spots)
            s = lax.broadcasted_iota(jnp.int32, (n, wide), 0)
            lane = lax.broadcasted_iota(jnp.int32, (n, wide), 1)
            down, across = jnp.zeros_like(s), jnp.zeros_like(s)
            for c, (a, b) in enumerate(spots):
                for h in range(heads):
                    place = order_ref[(h * inners + a) * outers + b]
                    down = jnp.where(s == c * heads + h, place, down)
                    across = jnp.where(lane == c * heads + h, place, across)
            ahead = jnp.where((across > down) & (lane < n), 1, 0)
            hit = jnp.sum(ahead, axis=1, keepdims=True) == lane
            ids = jnp.sum(jnp.where(hit, s, 0), axis=0, keepdims=True)
            return ids, jnp.sum(jnp.where(hit, down, 0), axis=0, keepdims=True)

        own, lists = spots_of()
        q_id, q_order = sort([own])
        rows = [q_id, q_order]
        lane = lax.broadcasted_iota(jnp.int32, (1, wide), 1)
        for spots in lists:
            ids, order = sort(spots)
            step = keys_step * len(spots)
            seen = jnp.zeros((1, wide), jnp.int32)
            for g in range(heads * len(spots) // step):
                least = jnp.sum(
                    jnp.where(lane == (g + 1) * step - 1, order, 0), axis=1, keepdims=True
                )
                count = jnp.sum(
                    jnp.where((q_order >= least) & (lane < heads), 1, 0), axis=1, keepdims=True
                )
                seen = jnp.where(lane == g, count, seen)
            rows += [ids, order, seen]
        rows.append(jnp.zeros((16 - len(rows), wide), jnp.int32))
        out_ref[...] = jnp.concatenate(rows, axis=0)

    return pl.pallas_call(
        body,
        out_shape=jax.ShapeDtypeStruct((16, wide), jnp.int32),
        in_specs=[pl.BlockSpec(memory_space=pltpu.SMEM)],
        out_specs=pl.BlockSpec(memory_space=pltpu.VMEM),
        compiler_params=PARAMS,
        name="order_tables",
    )(block_order)


def pieces(x):
    high = lax.reduce_precision(x, 8, 7)
    rest = x - high
    middle = lax.reduce_precision(rest, 8, 7)
    return [v.astype(bf16) for v in (high, middle, rest - middle)]


def shards(query, keys, values, attn_out, grad_out, log_norm, block_order):
    heads = lax.axis_size("head")
    inners = lax.axis_size("inner")
    outers = lax.axis_size("outer")
    T, q_heads, D = query.shape
    group = q_heads // keys.shape[1]

    ring = ("inner", "outer")
    place = lambda a, b: a * outers + b
    swap = [(place(1 - a, b), place(a, b)) for a in range(inners) for b in range(outers)]
    ahead = [
        (place(a, b), place(a, b + 1) if b + 1 < outers else place(1 - a, 0))
        for a in range(inners)
        for b in range(outers)
    ]
    across = [(dict(swap)[a], b) for a, b in ahead]
    back = [(b, a) for a, b in ahead]

    def exchange(x):
        return lax.all_to_all(x, "head", split_axis=0, concat_axis=0, tiled=True)

    def by_head(x):
        return x.reshape(T, heads, -1, D).transpose(1, 2, 0, 3)

    kv = exchange(jnp.concatenate([by_head(keys), by_head(values)], axis=1))
    kv_far_partner = lax.ppermute(kv, ring, across)
    kv_far = lax.ppermute(kv, ring, ahead)
    kv_after, kv_far_partner = lax.optimization_barrier((kv, kv_far_partner))
    kv_partner = lax.ppermute(kv_after, ring, swap)

    delta = jnp.sum(grad_out.astype(f32) * attn_out.astype(f32), axis=-1)
    stats = jnp.stack([log_norm * LOG2E, delta])
    lanes = group * T // D
    stats = stats.reshape(2, T, heads, group).transpose(2, 0, 3, 1).reshape(heads, 2 * lanes, D)
    stats = jnp.pad(stats, ((0, 0), (0, 8 - 2 * lanes), (0, 0)))
    stats = jnp.concatenate(pieces(stats), axis=1)
    stats = jnp.pad(stats, ((0, 0), (0, 8), (0, 0)))
    keys_step, rows_step = 4, 4
    names = ["far_partner", "far", "near_partner", "near"]

    def spots_of():
        a, b = lax.axis_index("inner"), lax.axis_index("outer")
        before = jnp.where(b == 0, outers - 1, b - 1)
        turn = jnp.where(b == 0, 1 - a, a)
        lists = [[(1 - turn, before)], [(turn, before)], [(1 - a, b)], [(a, b)]]
        return (a, b), lists

    tables = order_tables(block_order, spots_of, heads, inners, outers, keys_step)
    rows_of = lambda x: by_head(x).reshape(heads, group * T, D)
    stats, tables = lax.optimization_barrier((stats, tables))
    packed = exchange(jnp.concatenate([rows_of(query), rows_of(grad_out), stats], axis=1))
    def part(name, contexts, dq_starts, last, g_types):
        return attention_part(
            tables,
            2 + 3 * names.index(name),
            packed,
            contexts,
            dq_starts,
            last,
            keys_step * len(contexts),
            rows_step,
            group,
            g_types,
            name,
        )

    def to_peers(blocks):
        return [blocks[0]] + [
            lax.ppermute(blocks[j], "head", [(h, h ^ j) for h in range(heads)])
            for j in range(1, heads)
        ]

    dq, far_partner = part("far_partner", [kv_far_partner], [], False, [bf16])
    far_partner = lax.ppermute(far_partner, ring, back)
    starts = [dq]
    packed, dq = lax.optimization_barrier((packed, dq))
    dq, far = part("far", [kv_far], [], False, [bf16])
    far = lax.ppermute(far, ring, back)
    starts.append(dq)
    packed, dq = lax.optimization_barrier((packed, dq))
    dq, near_partner = part("near_partner", [kv_partner], starts, False, [f32])
    partner = (near_partner + far_partner.astype(f32)).astype(bf16)
    partner = lax.ppermute(partner, ring, swap)
    dq, near = part("near", [kv], [dq], True, [f32])
    dq = exchange(dq)
    grad = to_peers(add_by_peer(near, partner, far))
    dq = dq.reshape(q_heads, T, D).transpose(1, 0, 2)
    dq, grad = lax.optimization_barrier((dq, grad))
    return dq, *gather_grads(grad)


def solution(mesh):
    rows = P(("head", "inner", "outer"))
    return jax.shard_map(
        shards,
        mesh=mesh,
        in_specs=(rows,) * 6 + (P(),),
        out_specs=(rows,) * 3,
        check_vma=False,
    )
```

```python
import math

import jax
import jax.numpy as jnp
from jax import lax
from jax.experimental import pallas as pl
from jax.experimental.pallas import tpu as pltpu
from jax.sharding import PartitionSpec as P

LOG2E = math.log2(math.e)
NT = (((1,), (1,)), ((), ()))
NN = (((1,), (0,)), ((), ()))
PARAMS = pltpu.CompilerParams(vmem_limit_bytes=32 * 2**20)
f32 = jnp.float32
bf16 = jnp.bfloat16


def attention_part(
    tables, row, packed, contexts, dq_starts, last, keys_step, rows_step, heads, g_types, name
):
    src, _, T, D = contexts[0].shape
    R = heads * T
    many = len(contexts)
    n = many * src
    U, W = keys_step * T, rows_step * R
    groups = n // keys_step
    scale = D ** (-0.5)
    lanes = R // D

    def body(table, packed_ref, *rest):
        kv_refs, rest = rest[:many], rest[many:]
        start_refs, rest = rest[: len(dq_starts)], rest[len(dq_starts) :]
        out_ref, *rest = rest
        g_refs, rest = rest[:many], rest[many:]
        if many > 1:
            kv_s, g_s, *rest = rest
            for c in range(many):
                kv_s[c * src : (c + 1) * src] = kv_refs[c][...]
        else:
            kv_s, g_s = kv_refs[0], g_refs[0]
        st_s, k_s, v_s, kt_s, dk_s, dv_s, *rest = rest
        dq_s = rest[0] if last else out_ref
        dq_s[...] = sum((r[...] for r in start_refs), jnp.zeros_like(dq_s))
        kid = lambda j: table[row, j]
        kord = lambda j: table[row + 1, j]

        def prepare(i, carry):
            st = packed_ref[table[0, i], 2 * R :].astype(f32)
            st = st[0:8] + st[8:16] + st[16:24]
            st_s[i, 0:1] = jnp.concatenate([st[j : j + 1] for j in range(lanes)], axis=1)
            st_s[i, 1:2] = jnp.concatenate([st[j : j + 1] for j in range(lanes, 2 * lanes)], axis=1)
            return carry

        lax.fori_loop(0, src, prepare, 0)
        lead = lax.broadcasted_iota(jnp.int32, (T, R), 1) % T - lax.broadcasted_iota(
            jnp.int32, (T, R), 0
        )

        def group(g, carry):
            for j in range(keys_step):
                b = kid(g * keys_step + j)
                k_s[pl.ds(j * T, T)] = kv_s[b, 0]
                v_s[pl.ds(j * T, T)] = kv_s[b, 1]
            kt_s[...] = k_s[...].T
            dk_s[...] = jnp.zeros_like(dk_s)
            dv_s[...] = jnp.zeros_like(dv_s)

            def step(i, inner):
                at = pl.ds(pl.multiple_of(i * W, W), W)
                ids = [table[0, i * rows_step + h] for h in range(rows_step)]
                q = jnp.concatenate([packed_ref[b, 0:R] for b in ids], axis=0)
                do = jnp.concatenate([packed_ref[b, R : 2 * R] for b in ids], axis=0)
                k, v = k_s[...], v_s[...]
                s = lax.dot_general(k, q, NT, preferred_element_type=f32)
                dp = lax.dot_general(v, do, NT, preferred_element_type=f32)
                p_cols, ds_cols = [], []
                for h in range(rows_step):
                    at_row = i * rows_step + h
                    lse, delta, place = st_s[at_row, 0:1], st_s[at_row, 1:2], table[1, at_row]
                    p_rows, ds_rows = [], []
                    for j in range(keys_step):
                        behind = (kord(g * keys_step + j) - place) * T
                        cut = (slice(j * T, (j + 1) * T), slice(h * R, (h + 1) * R))
                        p = jnp.where(
                            lead >= behind, jnp.exp2(s[cut] * (scale * LOG2E) - lse), 0.0
                        )
                        ds_rows.append((p * (dp[cut] - delta)).astype(bf16))
                        p_rows.append(p.astype(bf16))
                    p_cols.append(jnp.concatenate(p_rows, axis=0))
                    ds_cols.append(jnp.concatenate(ds_rows, axis=0))
                p, ds = jnp.concatenate(p_cols, axis=1), jnp.concatenate(ds_cols, axis=1)
                dv_s[...] += lax.dot_general(p, do, NN, preferred_element_type=f32)
                dk_s[...] += lax.dot_general(ds, q, NN, preferred_element_type=f32)
                dq_s[:, at] += lax.dot_general(kt_s[...], ds, NN, preferred_element_type=f32)
                return inner

            steps = (table[row + 2, g] + rows_step - 1) // rows_step
            lax.fori_loop(0, steps, step, 0)
            for j in range(keys_step):
                b = kid(g * keys_step + j)
                g_s[b, 0] = (dk_s[pl.ds(j * T, T)] * scale).astype(g_s.dtype)
                g_s[b, 1] = dv_s[pl.ds(j * T, T)].astype(g_s.dtype)
            return carry

        lax.fori_loop(0, groups, group, 0)
        if many > 1:
            for c in range(many):
                g_refs[c][...] = g_s[c * src : (c + 1) * src].astype(g_refs[c].dtype)
        if last:
            stage, sems = rest[1:]
            copies = []
            for j in range(src):
                stage[j] = (dq_s[:, j * R : (j + 1) * R] * scale).astype(bf16).T
                copies.append(
                    pltpu.make_async_copy(stage.at[j], out_ref.at[table[0, j]], sems.at[j])
                )
                copies[-1].start()
            for copy in copies:
                copy.wait()

    smem = pl.BlockSpec(memory_space=pltpu.SMEM)
    vmem = pl.BlockSpec(memory_space=pltpu.VMEM)
    if last:
        dq_out = jax.ShapeDtypeStruct((src, R, D), bf16)
    else:
        dq_out = jax.ShapeDtypeStruct((D, src * R), f32)
    g_outs = [jax.ShapeDtypeStruct((src, 2, T, D), t) for t in g_types]
    scratch = []
    if many > 1:
        scratch = [pltpu.VMEM((n, 2, T, D), bf16), pltpu.VMEM((n, 2, T, D), f32)]
    scratch += [
        pltpu.VMEM((src, 8, R), f32),
        pltpu.VMEM((U, D), bf16),
        pltpu.VMEM((U, D), bf16),
        pltpu.VMEM((D, U), bf16),
        pltpu.VMEM((U, D), f32),
        pltpu.VMEM((U, D), f32),
    ]
    if last:
        scratch += [
            pltpu.VMEM((D, src * R), f32),
            pltpu.VMEM((src, R, D), bf16),
            pltpu.SemaphoreType.DMA((src,)),
        ]
    arrays = [packed, *contexts, *dq_starts]
    return pl.pallas_call(
        body,
        out_shape=(dq_out, *g_outs),
        in_specs=[smem] + [vmem] * len(arrays),
        out_specs=(pl.BlockSpec(memory_space=pltpu.HBM) if last else vmem,) + (vmem,) * many,
        scratch_shapes=scratch,
        compiler_params=PARAMS,
        cost_estimate=pl.CostEstimate(flops=1, bytes_accessed=1, transcendentals=0),
        name=name,
    )(tables, *arrays)


def add_by_peer(*arrays):
    src, *rest = arrays[0].shape

    def body(*refs):
        ins, outs = refs[: len(arrays)], refs[len(arrays) :]
        me = lax.axis_index("head")
        for j in range(src):
            at = me ^ j
            outs[j % 2][j // 2] = sum(r[at].astype(f32) for r in ins).astype(bf16)

    vmem = pl.BlockSpec(memory_space=pltpu.VMEM)
    return pl.pallas_call(
        body,
        out_shape=[jax.ShapeDtypeStruct((src // 2, *rest), bf16)] * 2,
        in_specs=[vmem] * len(arrays),
        out_specs=[vmem] * 2,
        cost_estimate=pl.CostEstimate(flops=10**10, bytes_accessed=1, transcendentals=0),
        compiler_params=PARAMS,
        name="add_by_peer",
    )(*arrays)


def pair_up(own, mate):
    n, *rest = own.shape

    def body(own_ref, mate_ref, *outs):
        for k in range(n):
            outs[k][0] = own_ref[k]
            outs[k][1] = mate_ref[k]

    vmem = pl.BlockSpec(memory_space=pltpu.VMEM)
    return pl.pallas_call(
        body,
        out_shape=[jax.ShapeDtypeStruct((2, *rest), own.dtype)] * n,
        in_specs=[vmem] * 2,
        out_specs=[vmem] * n,
        compiler_params=PARAMS,
        name="pair_up",
    )(own, mate)


def gather_grads(pairs):
    src = 2 * len(pairs)
    _, _, T, D = pairs[0].shape

    def body(*refs):
        me = lax.axis_index("head")
        ins, outs, held, wide = refs[: src // 2], refs[src // 2 : src // 2 + 2], refs[-2], refs[-1]
        for j in range(src):
            held[me ^ j] = ins[j // 2][j % 2]
        for c in range(2):
            for g in range(src):
                wide[:, g, :] = held[g, c].astype(f32)
            outs[c][...] = wide[...].astype(bf16)

    vmem = pl.BlockSpec(memory_space=pltpu.VMEM)
    return pl.pallas_call(
        body,
        out_shape=[jax.ShapeDtypeStruct((T, src, D), bf16)] * 2,
        in_specs=[vmem] * (src // 2),
        out_specs=[vmem] * 2,
        scratch_shapes=[pltpu.VMEM((src, 2, T, D), bf16), pltpu.VMEM((T, src, D), f32)],
        compiler_params=PARAMS,
        name="gather_grads",
    )(*pairs)


def order_tables(block_order, spots_of, heads, inners, outers, keys_step):
    wide = 128

    def body(order_ref, out_ref):
        def sort(spots):
            n = heads * len(spots)
            s = lax.broadcasted_iota(jnp.int32, (n, wide), 0)
            lane = lax.broadcasted_iota(jnp.int32, (n, wide), 1)
            down, across = jnp.zeros_like(s), jnp.zeros_like(s)
            for c, (a, b) in enumerate(spots):
                for h in range(heads):
                    place = order_ref[(h * inners + a) * outers + b]
                    down = jnp.where(s == c * heads + h, place, down)
                    across = jnp.where(lane == c * heads + h, place, across)
            ahead = jnp.where((across > down) & (lane < n), 1, 0)
            hit = jnp.sum(ahead, axis=1, keepdims=True) == lane
            ids = jnp.sum(jnp.where(hit, s, 0), axis=0, keepdims=True)
            return ids, jnp.sum(jnp.where(hit, down, 0), axis=0, keepdims=True)

        own, lists = spots_of()
        q_id, q_order = sort([own])
        rows = [q_id, q_order]
        lane = lax.broadcasted_iota(jnp.int32, (1, wide), 1)
        for spots in lists:
            ids, order = sort(spots)
            step = keys_step * len(spots)
            seen = jnp.zeros((1, wide), jnp.int32)
            for g in range(heads * len(spots) // step):
                least = jnp.sum(
                    jnp.where(lane == (g + 1) * step - 1, order, 0), axis=1, keepdims=True
                )
                count = jnp.sum(
                    jnp.where((q_order >= least) & (lane < heads), 1, 0), axis=1, keepdims=True
                )
                seen = jnp.where(lane == g, count, seen)
            rows += [ids, order, seen]
        rows.append(jnp.zeros((16 - len(rows), wide), jnp.int32))
        out_ref[...] = jnp.concatenate(rows, axis=0)

    return pl.pallas_call(
        body,
        out_shape=jax.ShapeDtypeStruct((16, wide), jnp.int32),
        in_specs=[pl.BlockSpec(memory_space=pltpu.SMEM)],
        out_specs=pl.BlockSpec(memory_space=pltpu.VMEM),
        compiler_params=PARAMS,
        name="order_tables",
    )(block_order)


def pieces(x):
    high = lax.reduce_precision(x, 8, 7)
    rest = x - high
    middle = lax.reduce_precision(rest, 8, 7)
    return [v.astype(bf16) for v in (high, middle, rest - middle)]


def shards(query, keys, values, attn_out, grad_out, log_norm, block_order):
    heads = lax.axis_size("head")
    inners = lax.axis_size("inner")
    outers = lax.axis_size("outer")
    T, q_heads, D = query.shape
    group = q_heads // keys.shape[1]

    ring = ("inner", "outer")
    place = lambda a, b: a * outers + b
    swap = [(place(1 - a, b), place(a, b)) for a in range(inners) for b in range(outers)]
    ahead = [
        (place(a, b), place(a, b + 1) if b + 1 < outers else place(1 - a, 0))
        for a in range(inners)
        for b in range(outers)
    ]
    across = [(dict(swap)[a], b) for a, b in ahead]
    back = [(b, a) for a, b in ahead]

    def exchange(x):
        return lax.all_to_all(x, "head", split_axis=0, concat_axis=0, tiled=True)

    def by_head(x):
        return x.reshape(T, heads, -1, D).transpose(1, 2, 0, 3)

    kv = exchange(jnp.concatenate([by_head(keys), by_head(values)], axis=1))
    kv_far_partner = lax.ppermute(kv, ring, across)
    kv_far = lax.ppermute(kv, ring, ahead)
    kv_after, kv_far_partner = lax.optimization_barrier((kv, kv_far_partner))
    kv_partner = lax.ppermute(kv_after, ring, swap)

    delta = jnp.sum(grad_out.astype(f32) * attn_out.astype(f32), axis=-1)
    stats = jnp.stack([log_norm * LOG2E, delta])
    lanes = group * T // D
    stats = stats.reshape(2, T, heads, group).transpose(2, 0, 3, 1).reshape(heads, 2 * lanes, D)
    stats = jnp.pad(stats, ((0, 0), (0, 8 - 2 * lanes), (0, 0)))
    stats = jnp.concatenate(pieces(stats), axis=1)
    stats = jnp.pad(stats, ((0, 0), (0, 8), (0, 0)))
    keys_step, rows_step = 4, 4
    names = ["far_partner", "far", "near_partner", "near"]

    def spots_of():
        a, b = lax.axis_index("inner"), lax.axis_index("outer")
        before = jnp.where(b == 0, outers - 1, b - 1)
        turn = jnp.where(b == 0, 1 - a, a)
        lists = [[(1 - turn, before)], [(turn, before)], [(1 - a, b)], [(a, b)]]
        return (a, b), lists

    tables = order_tables(block_order, spots_of, heads, inners, outers, keys_step)
    rows_of = lambda x: by_head(x).reshape(heads, group * T, D)
    stats, tables = lax.optimization_barrier((stats, tables))
    packed = exchange(jnp.concatenate([rows_of(query), rows_of(grad_out), stats], axis=1))
    def part(name, contexts, dq_starts, last, g_types):
        return attention_part(
            tables,
            2 + 3 * names.index(name),
            packed,
            contexts,
            dq_starts,
            last,
            keys_step * len(contexts),
            rows_step,
            group,
            g_types,
            name,
        )

    def to_head(x, turn):
        return lax.ppermute(x, "head", [(h, h ^ turn) for h in range(heads)])

    dq, far_partner = part("far_partner", [kv_far_partner], [], False, [bf16])
    far_partner = lax.ppermute(far_partner, ring, back)
    starts = [dq]
    packed, dq = lax.optimization_barrier((packed, dq))
    dq, far = part("far", [kv_far], [], False, [bf16])
    far = lax.ppermute(far, ring, back)
    starts.append(dq)
    packed, dq = lax.optimization_barrier((packed, dq))
    dq, near_partner = part("near_partner", [kv_partner], starts, False, [f32])
    partner = (near_partner + far_partner.astype(f32)).astype(bf16)
    partner = lax.ppermute(partner, ring, swap)
    dq, near = part("near", [kv], [dq], True, [f32])
    dq = exchange(dq)
    own, mate = add_by_peer(near, partner, far)
    pairs = pair_up(own, to_head(mate, 1))
    grad = [pairs[0]] + [to_head(pairs[k], 2 * k) for k in range(1, heads // 2)]
    dq = dq.reshape(q_heads, T, D).transpose(1, 0, 2)
    dq, grad = lax.optimization_barrier((dq, grad))
    return dq, *gather_grads(grad)


def solution(mesh):
    rows = P(("head", "inner", "outer"))
    return jax.shard_map(
        shards,
        mesh=mesh,
        in_specs=(rows,) * 6 + (P(),),
        out_specs=(rows,) * 3,
        check_vma=False,
    )
```

```python
import math

import jax
import jax.numpy as jnp
from jax import lax
from jax.experimental import pallas as pl
from jax.experimental.pallas import tpu as pltpu
from jax.sharding import PartitionSpec as P

LOG2E = math.log2(math.e)
NT = (((1,), (1,)), ((), ()))
NN = (((1,), (0,)), ((), ()))
PARAMS = pltpu.CompilerParams(vmem_limit_bytes=32 * 2**20)
f32 = jnp.float32
bf16 = jnp.bfloat16


def attention_part(
    tables, row, packed, contexts, dq_starts, last, keys_step, rows_step, heads, g_types, name
):
    src, _, T, D = contexts[0].shape
    R = heads * T
    many = len(contexts)
    n = many * src
    U, W = keys_step * T, rows_step * R
    groups = n // keys_step
    scale = D ** (-0.5)
    lanes = R // D

    def body(table, packed_ref, *rest):
        kv_refs, rest = rest[:many], rest[many:]
        start_refs, rest = rest[: len(dq_starts)], rest[len(dq_starts) :]
        out_ref, *rest = rest
        g_refs, rest = rest[:many], rest[many:]
        if many > 1:
            kv_s, g_s, *rest = rest
            for c in range(many):
                kv_s[c * src : (c + 1) * src] = kv_refs[c][...]
        else:
            kv_s, g_s = kv_refs[0], g_refs[0]
        st_s, k_s, v_s, kt_s, dk_s, dv_s, *rest = rest
        dq_s = rest[0] if last else out_ref
        dq_s[...] = sum((r[...] for r in start_refs), jnp.zeros_like(dq_s))
        kid = lambda j: table[row, j]
        kord = lambda j: table[row + 1, j]

        def prepare(i, carry):
            st = packed_ref[table[0, i], 2 * R :].astype(f32)
            st = st[0:8] + st[8:16] + st[16:24]
            st_s[i, 0:1] = jnp.concatenate([st[j : j + 1] for j in range(lanes)], axis=1)
            st_s[i, 1:2] = jnp.concatenate([st[j : j + 1] for j in range(lanes, 2 * lanes)], axis=1)
            return carry

        lax.fori_loop(0, src, prepare, 0)
        lead = lax.broadcasted_iota(jnp.int32, (T, R), 1) % T - lax.broadcasted_iota(
            jnp.int32, (T, R), 0
        )

        def group(g, carry):
            for j in range(keys_step):
                b = kid(g * keys_step + j)
                k_s[pl.ds(j * T, T)] = kv_s[b, 0]
                v_s[pl.ds(j * T, T)] = kv_s[b, 1]
            kt_s[...] = k_s[...].T
            dk_s[...] = jnp.zeros_like(dk_s)
            dv_s[...] = jnp.zeros_like(dv_s)

            def step(i, inner):
                at = pl.ds(pl.multiple_of(i * W, W), W)
                ids = [table[0, i * rows_step + h] for h in range(rows_step)]
                q = jnp.concatenate([packed_ref[b, 0:R] for b in ids], axis=0)
                do = jnp.concatenate([packed_ref[b, R : 2 * R] for b in ids], axis=0)
                k, v = k_s[...], v_s[...]
                s = lax.dot_general(k, q, NT, preferred_element_type=f32)
                dp = lax.dot_general(v, do, NT, preferred_element_type=f32)
                p_cols, ds_cols = [], []
                for h in range(rows_step):
                    at_row = i * rows_step + h
                    lse, delta, place = st_s[at_row, 0:1], st_s[at_row, 1:2], table[1, at_row]
                    p_rows, ds_rows = [], []
                    for j in range(keys_step):
                        behind = (kord(g * keys_step + j) - place) * T
                        cut = (slice(j * T, (j + 1) * T), slice(h * R, (h + 1) * R))
                        shift = lse if last else lse + jnp.where(behind > 0, 1e30, 0.0)
                        p = jnp.exp2(s[cut] * (scale * LOG2E) - shift)
                        if last:
                            p = jnp.where(lead >= behind, p, 0.0)
                        ds_rows.append((p * (dp[cut] - delta)).astype(bf16))
                        p_rows.append(p.astype(bf16))
                    p_cols.append(jnp.concatenate(p_rows, axis=0))
                    ds_cols.append(jnp.concatenate(ds_rows, axis=0))
                p, ds = jnp.concatenate(p_cols, axis=1), jnp.concatenate(ds_cols, axis=1)
                dv_s[...] += lax.dot_general(p, do, NN, preferred_element_type=f32)
                dk_s[...] += lax.dot_general(ds, q, NN, preferred_element_type=f32)
                dq_s[:, at] += lax.dot_general(kt_s[...], ds, NN, preferred_element_type=f32)
                return inner

            steps = (table[row + 2, g] + rows_step - 1) // rows_step
            lax.fori_loop(0, steps, step, 0)
            for j in range(keys_step):
                b = kid(g * keys_step + j)
                g_s[b, 0] = (dk_s[pl.ds(j * T, T)] * scale).astype(g_s.dtype)
                g_s[b, 1] = dv_s[pl.ds(j * T, T)].astype(g_s.dtype)
            return carry

        lax.fori_loop(0, groups, group, 0)
        if many > 1:
            for c in range(many):
                g_refs[c][...] = g_s[c * src : (c + 1) * src].astype(g_refs[c].dtype)
        if last:
            stage, sems = rest[1:]
            copies = []
            for j in range(src):
                stage[j] = (dq_s[:, j * R : (j + 1) * R] * scale).astype(bf16).T
                copies.append(
                    pltpu.make_async_copy(stage.at[j], out_ref.at[table[0, j]], sems.at[j])
                )
                copies[-1].start()
            for copy in copies:
                copy.wait()

    smem = pl.BlockSpec(memory_space=pltpu.SMEM)
    vmem = pl.BlockSpec(memory_space=pltpu.VMEM)
    if last:
        dq_out = jax.ShapeDtypeStruct((src, R, D), bf16)
    else:
        dq_out = jax.ShapeDtypeStruct((D, src * R), f32)
    g_outs = [jax.ShapeDtypeStruct((src, 2, T, D), t) for t in g_types]
    scratch = []
    if many > 1:
        scratch = [pltpu.VMEM((n, 2, T, D), bf16), pltpu.VMEM((n, 2, T, D), f32)]
    scratch += [
        pltpu.VMEM((src, 8, R), f32),
        pltpu.VMEM((U, D), bf16),
        pltpu.VMEM((U, D), bf16),
        pltpu.VMEM((D, U), bf16),
        pltpu.VMEM((U, D), f32),
        pltpu.VMEM((U, D), f32),
    ]
    if last:
        scratch += [
            pltpu.VMEM((D, src * R), f32),
            pltpu.VMEM((src, R, D), bf16),
            pltpu.SemaphoreType.DMA((src,)),
        ]
    arrays = [packed, *contexts, *dq_starts]
    return pl.pallas_call(
        body,
        out_shape=(dq_out, *g_outs),
        in_specs=[smem] + [vmem] * len(arrays),
        out_specs=(pl.BlockSpec(memory_space=pltpu.HBM) if last else vmem,) + (vmem,) * many,
        scratch_shapes=scratch,
        compiler_params=PARAMS,
        cost_estimate=pl.CostEstimate(flops=1, bytes_accessed=1, transcendentals=0),
        name=name,
    )(tables, *arrays)


def add_by_peer(*arrays):
    src, *rest = arrays[0].shape

    def body(*refs):
        ins, outs = refs[: len(arrays)], refs[len(arrays) :]
        me = lax.axis_index("head")
        for j in range(src):
            at = me ^ j
            outs[j % 2][j // 2] = sum(r[at].astype(f32) for r in ins).astype(bf16)

    vmem = pl.BlockSpec(memory_space=pltpu.VMEM)
    return pl.pallas_call(
        body,
        out_shape=[jax.ShapeDtypeStruct((src // 2, *rest), bf16)] * 2,
        in_specs=[vmem] * len(arrays),
        out_specs=[vmem] * 2,
        cost_estimate=pl.CostEstimate(flops=10**10, bytes_accessed=1, transcendentals=0),
        compiler_params=PARAMS,
        name="add_by_peer",
    )(*arrays)


def pair_up(own, mate):
    n, *rest = own.shape

    def body(own_ref, mate_ref, *outs):
        for k in range(n):
            outs[k][0] = own_ref[k]
            outs[k][1] = mate_ref[k]

    vmem = pl.BlockSpec(memory_space=pltpu.VMEM)
    return pl.pallas_call(
        body,
        out_shape=[jax.ShapeDtypeStruct((2, *rest), own.dtype)] * n,
        in_specs=[vmem] * 2,
        out_specs=[vmem] * n,
        compiler_params=PARAMS,
        name="pair_up",
    )(own, mate)


def gather_grads(pairs):
    src = 2 * len(pairs)
    _, _, T, D = pairs[0].shape

    def body(*refs):
        me = lax.axis_index("head")
        ins, outs, held, wide = refs[: src // 2], refs[src // 2 : src // 2 + 2], refs[-2], refs[-1]
        for j in range(src):
            held[me ^ j] = ins[j // 2][j % 2]
        for c in range(2):
            for g in range(src):
                wide[:, g, :] = held[g, c].astype(f32)
            outs[c][...] = wide[...].astype(bf16)

    vmem = pl.BlockSpec(memory_space=pltpu.VMEM)
    return pl.pallas_call(
        body,
        out_shape=[jax.ShapeDtypeStruct((T, src, D), bf16)] * 2,
        in_specs=[vmem] * (src // 2),
        out_specs=[vmem] * 2,
        scratch_shapes=[pltpu.VMEM((src, 2, T, D), bf16), pltpu.VMEM((T, src, D), f32)],
        compiler_params=PARAMS,
        name="gather_grads",
    )(*pairs)


def order_tables(block_order, spots_of, heads, inners, outers, keys_step):
    wide = 128

    def body(order_ref, out_ref):
        def sort(spots):
            n = heads * len(spots)
            s = lax.broadcasted_iota(jnp.int32, (n, wide), 0)
            lane = lax.broadcasted_iota(jnp.int32, (n, wide), 1)
            down, across = jnp.zeros_like(s), jnp.zeros_like(s)
            for c, (a, b) in enumerate(spots):
                for h in range(heads):
                    place = order_ref[(h * inners + a) * outers + b]
                    down = jnp.where(s == c * heads + h, place, down)
                    across = jnp.where(lane == c * heads + h, place, across)
            ahead = jnp.where((across > down) & (lane < n), 1, 0)
            hit = jnp.sum(ahead, axis=1, keepdims=True) == lane
            ids = jnp.sum(jnp.where(hit, s, 0), axis=0, keepdims=True)
            return ids, jnp.sum(jnp.where(hit, down, 0), axis=0, keepdims=True)

        own, lists = spots_of()
        q_id, q_order = sort([own])
        rows = [q_id, q_order]
        lane = lax.broadcasted_iota(jnp.int32, (1, wide), 1)
        for spots in lists:
            ids, order = sort(spots)
            step = keys_step * len(spots)
            seen = jnp.zeros((1, wide), jnp.int32)
            for g in range(heads * len(spots) // step):
                least = jnp.sum(
                    jnp.where(lane == (g + 1) * step - 1, order, 0), axis=1, keepdims=True
                )
                count = jnp.sum(
                    jnp.where((q_order >= least) & (lane < heads), 1, 0), axis=1, keepdims=True
                )
                seen = jnp.where(lane == g, count, seen)
            rows += [ids, order, seen]
        rows.append(jnp.zeros((16 - len(rows), wide), jnp.int32))
        out_ref[...] = jnp.concatenate(rows, axis=0)

    return pl.pallas_call(
        body,
        out_shape=jax.ShapeDtypeStruct((16, wide), jnp.int32),
        in_specs=[pl.BlockSpec(memory_space=pltpu.SMEM)],
        out_specs=pl.BlockSpec(memory_space=pltpu.VMEM),
        compiler_params=PARAMS,
        name="order_tables",
    )(block_order)


def pieces(x):
    high = lax.reduce_precision(x, 8, 7)
    rest = x - high
    middle = lax.reduce_precision(rest, 8, 7)
    return [v.astype(bf16) for v in (high, middle, rest - middle)]


def shards(query, keys, values, attn_out, grad_out, log_norm, block_order):
    heads = lax.axis_size("head")
    inners = lax.axis_size("inner")
    outers = lax.axis_size("outer")
    T, q_heads, D = query.shape
    group = q_heads // keys.shape[1]

    ring = ("inner", "outer")
    place = lambda a, b: a * outers + b
    swap = [(place(1 - a, b), place(a, b)) for a in range(inners) for b in range(outers)]
    ahead = [
        (place(a, b), place(a, b + 1) if b + 1 < outers else place(1 - a, 0))
        for a in range(inners)
        for b in range(outers)
    ]
    across = [(dict(swap)[a], b) for a, b in ahead]
    back = [(b, a) for a, b in ahead]

    def exchange(x):
        return lax.all_to_all(x, "head", split_axis=0, concat_axis=0, tiled=True)

    def by_head(x):
        return x.reshape(T, heads, -1, D).transpose(1, 2, 0, 3)

    kv = exchange(jnp.concatenate([by_head(keys), by_head(values)], axis=1))
    kv_far_partner = lax.ppermute(kv, ring, across)
    kv_far = lax.ppermute(kv, ring, ahead)
    kv_after, kv_far_partner = lax.optimization_barrier((kv, kv_far_partner))
    kv_partner = lax.ppermute(kv_after, ring, swap)

    delta = jnp.sum(grad_out.astype(f32) * attn_out.astype(f32), axis=-1)
    stats = jnp.stack([log_norm * LOG2E, delta])
    lanes = group * T // D
    stats = stats.reshape(2, T, heads, group).transpose(2, 0, 3, 1).reshape(heads, 2 * lanes, D)
    stats = jnp.pad(stats, ((0, 0), (0, 8 - 2 * lanes), (0, 0)))
    stats = jnp.concatenate(pieces(stats), axis=1)
    stats = jnp.pad(stats, ((0, 0), (0, 8), (0, 0)))
    keys_step, rows_step = 4, 4
    names = ["far_partner", "far", "near_partner", "near"]

    def spots_of():
        a, b = lax.axis_index("inner"), lax.axis_index("outer")
        before = jnp.where(b == 0, outers - 1, b - 1)
        turn = jnp.where(b == 0, 1 - a, a)
        lists = [[(1 - turn, before)], [(turn, before)], [(1 - a, b)], [(a, b)]]
        return (a, b), lists

    tables = order_tables(block_order, spots_of, heads, inners, outers, keys_step)
    rows_of = lambda x: by_head(x).reshape(heads, group * T, D)
    stats, tables = lax.optimization_barrier((stats, tables))
    packed = exchange(jnp.concatenate([rows_of(query), rows_of(grad_out), stats], axis=1))
    def part(name, contexts, dq_starts, last, g_types):
        return attention_part(
            tables,
            2 + 3 * names.index(name),
            packed,
            contexts,
            dq_starts,
            last,
            keys_step * len(contexts),
            rows_step,
            group,
            g_types,
            name,
        )

    def to_head(x, turn):
        return lax.ppermute(x, "head", [(h, h ^ turn) for h in range(heads)])

    dq, far_partner = part("far_partner", [kv_far_partner], [], False, [bf16])
    far_partner = lax.ppermute(far_partner, ring, back)
    starts = [dq]
    packed, dq = lax.optimization_barrier((packed, dq))
    dq, far = part("far", [kv_far], [], False, [bf16])
    far = lax.ppermute(far, ring, back)
    starts.append(dq)
    packed, dq = lax.optimization_barrier((packed, dq))
    dq, near_partner = part("near_partner", [kv_partner], starts, False, [f32])
    partner = (near_partner + far_partner.astype(f32)).astype(bf16)
    partner = lax.ppermute(partner, ring, swap)
    dq, near = part("near", [kv], [dq], True, [f32])
    dq = exchange(dq)
    own, mate = add_by_peer(near, partner, far)
    pairs = pair_up(own, to_head(mate, 1))
    grad = [pairs[0]] + [to_head(pairs[k], 2 * k) for k in range(1, heads // 2)]
    dq = dq.reshape(q_heads, T, D).transpose(1, 0, 2)
    dq, grad = lax.optimization_barrier((dq, grad))
    return dq, *gather_grads(grad)


def solution(mesh):
    rows = P(("head", "inner", "outer"))
    return jax.shard_map(
        shards,
        mesh=mesh,
        in_specs=(rows,) * 6 + (P(),),
        out_specs=(rows,) * 3,
        check_vma=False,
    )
```
